768 devices in a mesh: row: 48 (over y_lo, z, core), col: 16 (over y_hi, x).
Axes of the slice: x: 4, y: 8 (y_hi: 4, y_lo: 2; y = y_hi * 2 + y_lo), z: 12, core: 2. Of those that a mesh axis runs over, the one named last changes fastest.
Arguments:
- df_blocks: bfloat16 [576, 576, 1024], P('row', 'col'), may hold values from -1 to 1
- amplitudes: bfloat16 [48, 576, 576], P(None, 'col'), may hold values from -0.009765625 to 0.009765625
Outputs:
- ladder_ab: float32 [576, 4, 48], P('row')
- ladder_ba: float32 [576, 4, 48], P('row')
The draws below stay inside these ranges and needn't reach their ends.
All inputs are finite; a program needn't handle non-finite values.
Results may differ from the reference program's by a relative error of at most 0.0029.
Values may be sent and summed in bfloat16 or wider, within the bound.
No kernel may reach another device: no remote copies, remote signals or barrier semaphores. Data moves between devices by JAX's collectives and lax.ppermute only.
A program may use at most 64 MiB of HBM per device.

```python
import jax
import jax.numpy as jnp
from jax import lax

NV = 576
NAUX = 1024
WIN = 4
PAIRS = 48
N_ROW = 48


def block_scale(own_key, dims, split, smallest, largest):
    def one(position, parts):
        steps = jax.random.uniform(jax.random.fold_in(jax.random.fold_in(own_key, 6), position), (parts,), jnp.float32, smallest / len(split), largest / len(split))
        return jnp.repeat(jnp.exp(steps), dims[position] // parts).reshape((-1,) + (1,) * (len(dims) - position - 1))

    loudness = one(*split[0])
    for cut in split[1:]:
        loudness = loudness * one(*cut)
    return loudness


def noise(key, extent, width, reach, cuts=(), held_as=jnp.bfloat16):
    drawn = jax.random.normal(key, extent, jnp.float32) * width
    if len(cuts) > 0:
        drawn = block_scale(key, extent, cuts, -0.22, 0.18) * drawn
    return jnp.clip(drawn, min=-reach, max=reach).astype(held_as)


def setup_inputs(seed: int = 0) -> dict:
    seeds = jax.random.split(jax.random.key(seed), 3)
    return {
        "df_blocks": noise(seeds[0], (NV, NV, NAUX), 32 ** -0.5, 1.0, ((0, 48), (1, 16))),
        "amplitudes": noise(seeds[1], (PAIRS, NV, NV), (NV * NV) ** -0.5, 0.009765625, ((1, 16),)),
    }


def reference(df_blocks, amplitudes):
    own_rows = NV // N_ROW
    blocks = df_blocks.reshape(N_ROW, own_rows, NV, NAUX)
    partner = jnp.roll(blocks[:, :WIN], -1, axis=0)
    amps_wide = amplitudes.astype(jnp.float32)

    def ladder_block(block_pair):
        resident, window_rows = block_pair
        v_tile = jnp.einsum("acq,jdq->ajcd", resident.astype(jnp.float32), window_rows.astype(jnp.float32), precision=lax.Precision.HIGHEST)
        v_tile = lax.optimization_barrier(v_tile.astype(jnp.bfloat16)).astype(jnp.float32)
        forward = jnp.einsum("ajcd,pcd->ajp", v_tile, amps_wide, precision=lax.Precision.HIGHEST)
        backward = jnp.einsum("ajcd,pdc->ajp", v_tile, amps_wide, precision=lax.Precision.HIGHEST)
        return forward, backward

    forward, backward = lax.map(ladder_block, (blocks, partner))
    return forward.reshape(NV, WIN, PAIRS), backward.reshape(NV, WIN, PAIRS)
```

```python
import functools

import jax
import jax.numpy as jnp
from jax import lax
from jax.experimental import pallas as pl
from jax.experimental.pallas import tpu as pltpu
from jax.sharding import PartitionSpec as P

WIN = 4
SIDE = 4
LANES = 128
CHUNKS = 6
GROUP = 4
HIGHEST = lax.Precision.HIGHEST
ROWS_BY_ROWS = (((1,), (1,)), ((), ()))


def moved(value, dx, dy):
    pairs = [(yh * SIDE + x, (yh + dy) % SIDE * SIDE + (x + dx) % SIDE) for yh in range(SIDE) for x in range(SIDE)]
    return lax.ppermute(value, "col", pairs)


def from_next_row(value):
    rows = lax.axis_size("row")
    return lax.ppermute(value, "row", [(source, (source - 1) % rows) for source in range(rows)])


def between_cores(value):
    rows = lax.axis_size("row")
    return lax.ppermute(value, "row", [(source, source ^ 1) for source in range(rows)])


def core_0_along_x_core_1_along_y(value, step):
    pairs = []
    for row in range(lax.axis_size("row")):
        for yh in range(SIDE):
            for x in range(SIDE):
                to = (yh, (x + step) % SIDE) if row % 2 == 0 else ((yh + step) % SIDE, x)
                pairs.append((row * SIDE * SIDE + yh * SIDE + x, row * SIDE * SIDE + to[0] * SIDE + to[1]))
    return lax.ppermute(value, ("row", "col"), pairs)


def pack_kernel(own_c, at_ref, amps_ref, sent_ref, own_ref):
    x, yh, core = at_ref[0], at_ref[1], at_ref[2]
    rows, nv = amps_ref.shape
    tail = SIDE * own_c - LANES
    part = rows // CHUNKS

    def source(n, kind, step):
        near, e = n // own_c, n % own_c
        ab = ((yh - near + SIDE) % SIDE) * SIDE + (x + step) % SIDE
        ba = ((yh + step) % SIDE) * SIDE + (x - near + SIDE) % SIDE
        return jnp.where(kind == 0, ab, ba) * own_c + e

    kinds = [(core, 1), (core, 2), (core, 3), (0, 0), (1, 0)]
    lane = lax.broadcasted_iota(jnp.int32, (1, LANES), 1)
    wanted = [source(lane, kind, step) for kind, step in kinds]
    ends = jnp.full((1, LANES), -1, jnp.int32)
    for i, (kind, step) in enumerate(kinds):
        here = (lane >= i * tail) & (lane < (i + 1) * tail)
        ends = jnp.where(here, source(lane - i * tail + LANES, kind, step), ends)
    wanted = jnp.concatenate(wanted + [ends], 1)
    chosen = lax.broadcasted_iota(jnp.int32, (nv, wanted.shape[1]), 0) == wanted
    chosen = jnp.where(chosen, 1.0, 0.0).astype(jnp.bfloat16)

    def one(k, carry):
        at = pl.multiple_of(k * part, 16)
        got = jnp.dot(amps_ref[pl.ds(at, part), :], chosen, preferred_element_type=jnp.float32)
        end = got[:, 5 * LANES :]
        for i in range(3):
            sent_ref[i, pl.ds(at, part), :] = got[:, i * LANES : (i + 1) * LANES].astype(jnp.bfloat16)
        for i in (3, 4):
            own_ref[i - 3, pl.ds(at, part), :LANES] = got[:, i * LANES : (i + 1) * LANES].astype(jnp.bfloat16)
            own_ref[i - 3, pl.ds(at, part), LANES:] = pltpu.roll(end, LANES - i * tail, 1)[:, :tail].astype(jnp.bfloat16)
        new = []
        for i in range(3):
            turned = pltpu.roll(end, (k * tail + LANES - i * tail) % LANES, 1)
            new.append(jnp.where((lane >= k * tail) & (lane < (k + 1) * tail), turned, carry[i]))
        return tuple(new)

    carry = tuple(jnp.zeros((part, LANES), jnp.float32) for _ in range(3))
    for k in range(CHUNKS):
        carry = one(k, carry)
    for i in range(3):
        sent_ref[i, rows:, :] = carry[i].astype(jnp.bfloat16)


def unpack_kernel(core_ref, own_ref, mine_ref, other_ref, ab_ref, ba_ref):
    core = core_ref[0]
    rows = ab_ref.shape[1]
    part = rows // CHUNKS
    tail = ab_ref.shape[2] - LANES

    def put(from_ref, to_ref):
        for s in range(3):
            to_ref[s + 1, :, :LANES] = from_ref[s, :rows, :]
            end = from_ref[s, rows:, :].astype(jnp.float32)
            for k in range(CHUNKS):
                turned = end if k == 0 else pltpu.roll(end, LANES - k * tail, 1)
                to_ref[s + 1, k * part : (k + 1) * part, LANES:] = turned[:, :tail].astype(jnp.bfloat16)

    ab_ref[0] = own_ref[0]
    ba_ref[0] = own_ref[1]

    @pl.when(core == 0)
    def _():
        put(mine_ref, ab_ref)
        put(other_ref, ba_ref)

    @pl.when(core == 1)
    def _():
        put(other_ref, ab_ref)
        put(mine_ref, ba_ref)


def one_hot(shape, row_of, column_of, dtype):
    row = lax.broadcasted_iota(jnp.int32, shape, 0)
    column = lax.broadcasted_iota(jnp.int32, shape, 1)
    return jnp.where(row_of(row) == column_of(column), 1.0, 0.0).astype(dtype)


def ladder_kernel(own_a, own_c, pairs_p, *refs):
    lines, partners = refs[:SIDE], refs[SIDE : 2 * SIDE]
    ab_ref, ba_ref, out_ref, window, tile, total = refs[2 * SIDE :]
    wide = SIDE * own_c
    high = GROUP * own_a
    for j in range(WIN):
        rows = 0.0
        for s in range(SIDE):
            place = one_hot((wide, WIN * own_c), lambda r: r - s * own_c, lambda c: jnp.where((c >= j * own_c) & (c < (j + 1) * own_c), c - j * own_c, -wide - 1), jnp.bfloat16)
            rows += jnp.dot(place, partners[s][...], preferred_element_type=jnp.float32)
        window[j] = rows.astype(jnp.bfloat16)
    total[...] = jnp.zeros_like(total)
    for s in range(SIDE):
        for j in range(WIN):
            v = lax.dot_general(lines[s][...], window[j], ROWS_BY_ROWS, preferred_element_type=jnp.float32)
            tile[:, j] = v.astype(jnp.bfloat16).reshape(own_c // GROUP, high, wide)

        def one(g, carry):
            v = tile[g].reshape(WIN * high, wide)
            at = pl.ds(pl.multiple_of(g * GROUP * pairs_p, 16), GROUP * pairs_p)
            for i, amps in enumerate((ab_ref, ba_ref)):
                total[i] += lax.dot_general(v, amps[s, at, :], ROWS_BY_ROWS, preferred_element_type=jnp.float32)
            return carry

        lax.fori_loop(0, own_c // GROUP, one, 0, unroll=True)
    shape = total.shape[1:]
    row = lax.broadcasted_iota(jnp.int32, shape, 0)
    column = lax.broadcasted_iota(jnp.int32, shape, 1)
    same = (row % high) // own_a == column // pairs_p
    fold = one_hot((own_a * WIN, shape[0]), lambda r: r, lambda c: (c % own_a) * WIN + c // high, jnp.float32)
    out = 0.0
    for i in range(2):
        to = one_hot((shape[1], LANES), lambda r: r % pairs_p + i * pairs_p, lambda c: c, jnp.float32)
        out += jnp.dot(jnp.where(same, total[i], 0.0), to, precision=HIGHEST, preferred_element_type=jnp.float32)
    out_ref[...] = jnp.dot(fold, out, precision=HIGHEST, preferred_element_type=jnp.float32)


def add_kernel(pairs_p, parts_ref, ab_ref, ba_ref):
    total = jnp.sum(parts_ref[...], axis=0)
    ab_ref[...] = total[:, :pairs_p]
    ba_ref[...] = pltpu.roll(total, LANES - pairs_p, 1)[:, :pairs_p]


def shards(df_blocks, amplitudes):
    own_a, own_c, aux = df_blocks.shape
    pairs_p, _, nv = amplitudes.shape
    bf16, f32 = jnp.bfloat16, jnp.float32
    vmem, smem = pl.BlockSpec(memory_space=pltpu.VMEM), pl.BlockSpec(memory_space=pltpu.SMEM)
    params = pltpu.CompilerParams(vmem_limit_bytes=48 * 1024 * 1024)
    rows, wide = own_c * pairs_p, SIDE * own_c
    place, core = lax.axis_index("col"), lax.axis_index("row") % 2
    at = jnp.stack([place % SIDE, place // SIDE, core]).astype(jnp.int32)

    partner = from_next_row(df_blocks[:WIN].reshape(WIN * own_c, aux))
    resident = jnp.transpose(df_blocks, (1, 0, 2)).reshape(own_c * own_a, aux)
    amps = jnp.transpose(amplitudes, (1, 0, 2)).reshape(rows, nv)
    sent, own = pl.pallas_call(
        functools.partial(pack_kernel, own_c),
        out_shape=(jax.ShapeDtypeStruct((3, rows + rows // CHUNKS, LANES), bf16), jax.ShapeDtypeStruct((2, rows, wide), bf16)),
        in_specs=[smem, vmem],
        out_specs=(vmem, vmem),
        compiler_params=params,
        name="pack",
    )(at, amps)
    mine = [core_0_along_x_core_1_along_y(sent[s - 1], s) for s in (1, 3, 2)]
    mine = jnp.stack([mine[0], mine[2], mine[1]])
    lines = [resident] + [moved(resident, s, 0) for s in (1, 2, 3)]
    partners = [partner] + [moved(partner, 0, s) for s in (1, 2, 3)]
    other = between_cores(mine)
    ab, ba = pl.pallas_call(
        unpack_kernel,
        out_shape=(jax.ShapeDtypeStruct((SIDE, rows, wide), bf16),) * 2,
        in_specs=[smem, vmem, vmem, vmem],
        out_specs=(vmem, vmem),
        compiler_params=params,
        name="unpack",
    )(at[2:], own, mine, other)
    ba = jnp.transpose(ba.reshape(wide, pairs_p, wide), (2, 1, 0)).reshape(SIDE, rows, wide)
    part = pl.pallas_call(
        functools.partial(ladder_kernel, own_a, own_c, pairs_p),
        out_shape=jax.ShapeDtypeStruct((own_a * WIN, LANES), f32),
        in_specs=[vmem] * (2 * SIDE + 2),
        out_specs=vmem,
        scratch_shapes=[
            pltpu.VMEM((WIN, wide, aux), bf16),
            pltpu.VMEM((own_c // GROUP, WIN, GROUP * own_a, wide), bf16),
            pltpu.VMEM((2, WIN * GROUP * own_a, GROUP * pairs_p), f32),
        ],
        compiler_params=params,
        name="ladders",
    )(*lines, *partners, ab, ba)
    parts = lax.all_to_all(jnp.broadcast_to(part, (SIDE * SIDE, *part.shape)), "col", 0, 0, tiled=True)
    ab, ba = pl.pallas_call(
        functools.partial(add_kernel, pairs_p),
        out_shape=(jax.ShapeDtypeStruct((own_a * WIN, pairs_p), f32),) * 2,
        in_specs=[vmem],
        out_specs=(vmem, vmem),
        compiler_params=params,
        name="add",
    )(parts)
    return ab.reshape(own_a, WIN, pairs_p), ba.reshape(own_a, WIN, pairs_p)


def solution(mesh):
    in_specs = (P("row", "col", None), P(None, "col", None))
    out_specs = (P("row", None, None), P("row", None, None))
    return jax.shard_map(shards, mesh=mesh, in_specs=in_specs, out_specs=out_specs, check_vma=False)
```

```python
import functools

import jax
import jax.numpy as jnp
from jax import lax
from jax.experimental import pallas as pl
from jax.experimental.pallas import tpu as pltpu
from jax.sharding import PartitionSpec as P

WIN = 4
SIDE = 4
LANES = 128
CHUNKS = 6
GROUP = 4
HIGHEST = lax.Precision.HIGHEST
ROWS_BY_ROWS = (((1,), (1,)), ((), ()))


def moved(value, dx, dy):
    pairs = []
    for row in range(lax.axis_size("row")):
        sign = 1 - 2 * (row % 2)
        for yh in range(SIDE):
            for x in range(SIDE):
                to = (yh + sign * dy) % SIDE * SIDE + (x + sign * dx) % SIDE
                pairs.append(((row * SIDE + yh) * SIDE + x, row * SIDE * SIDE + to))
    return lax.ppermute(value, ("row", "col"), pairs)


def gathered(value, dx, dy):
    first = moved(value, dx, dy)
    return [value, first, moved(first, dx, dy), moved(value, -dx, -dy)]


def from_next_row(value):
    rows = lax.axis_size("row")
    return lax.ppermute(value, "row", [(source, (source - 1) % rows) for source in range(rows)])


def between_cores(value):
    rows = lax.axis_size("row")
    return lax.ppermute(value, "row", [(source, source ^ 1) for source in range(rows)])


def core_0_along_x_core_1_along_y(value, step):
    pairs = []
    for row in range(lax.axis_size("row")):
        for yh in range(SIDE):
            for x in range(SIDE):
                to = (yh, (x + step) % SIDE) if row % 2 == 0 else ((yh + step) % SIDE, x)
                pairs.append((row * SIDE * SIDE + yh * SIDE + x, row * SIDE * SIDE + to[0] * SIDE + to[1]))
    return lax.ppermute(value, ("row", "col"), pairs)


def pack_kernel(own_c, at_ref, amps_ref, before_1, before_2, sent_ref, own_ref):
    x, yh, core = at_ref[0], at_ref[1], at_ref[2]
    rows, nv = amps_ref.shape
    tail = SIDE * own_c - LANES
    part = rows // CHUNKS

    def source(n, kind, step):
        near, e = n // own_c, n % own_c
        ab = ((yh - near + SIDE) % SIDE) * SIDE + (x + step) % SIDE
        ba = ((yh + step) % SIDE) * SIDE + (x - near + SIDE) % SIDE
        return jnp.where(kind == 0, ab, ba) * own_c + e

    kinds = [(core, 1), (core, 2), (core, 3), (0, 0), (1, 0)]
    lane = lax.broadcasted_iota(jnp.int32, (1, LANES), 1)
    wanted = [source(lane, kind, step) for kind, step in kinds]
    ends = jnp.full((1, LANES), -1, jnp.int32)
    for i, (kind, step) in enumerate(kinds):
        here = (lane >= i * tail) & (lane < (i + 1) * tail)
        ends = jnp.where(here, source(lane - i * tail + LANES, kind, step), ends)
    wanted = jnp.concatenate(wanted + [ends], 1)
    chosen = lax.broadcasted_iota(jnp.int32, (nv, wanted.shape[1]), 0) == wanted
    chosen = jnp.where(chosen, 1.0, 0.0).astype(jnp.bfloat16)

    def one(k, carry):
        at = pl.multiple_of(k * part, 16)
        got = jnp.dot(amps_ref[pl.ds(at, part), :], chosen, preferred_element_type=jnp.float32)
        end = got[:, 5 * LANES :]
        for i in range(3):
            sent_ref[i, pl.ds(at, part), :] = got[:, i * LANES : (i + 1) * LANES].astype(jnp.bfloat16)
        for i in (3, 4):
            own_ref[i - 3, pl.ds(at, part), :LANES] = got[:, i * LANES : (i + 1) * LANES].astype(jnp.bfloat16)
            own_ref[i - 3, pl.ds(at, part), LANES:] = pltpu.roll(end, LANES - i * tail, 1)[:, :tail].astype(jnp.bfloat16)
        new = []
        for i in range(3):
            turned = pltpu.roll(end, (k * tail + LANES - i * tail) % LANES, 1)
            new.append(jnp.where((lane >= k * tail) & (lane < (k + 1) * tail), turned, carry[i]))
        return tuple(new)

    carry = tuple(jnp.zeros((part, LANES), jnp.float32) for _ in range(3))
    for k in range(CHUNKS):
        carry = one(k, carry)
    for i in range(3):
        sent_ref[i, rows:, :] = carry[i].astype(jnp.bfloat16)


def unpack_kernel(core_ref, own_ref, mine_ref, other_ref, ab_ref, ba_ref):
    core = core_ref[0]
    rows = ab_ref.shape[1]
    part = rows // CHUNKS
    tail = ab_ref.shape[2] - LANES

    def put(from_ref, to_ref):
        for s in range(3):
            to_ref[s + 1, :, :LANES] = from_ref[s, :rows, :]
            end = from_ref[s, rows:, :].astype(jnp.float32)
            for k in range(CHUNKS):
                turned = end if k == 0 else pltpu.roll(end, LANES - k * tail, 1)
                to_ref[s + 1, k * part : (k + 1) * part, LANES:] = turned[:, :tail].astype(jnp.bfloat16)

    ab_ref[0] = own_ref[0]
    ba_ref[0] = own_ref[1]

    @pl.when(core == 0)
    def _():
        put(mine_ref, ab_ref)
        put(other_ref, ba_ref)

    @pl.when(core == 1)
    def _():
        put(other_ref, ab_ref)
        put(mine_ref, ba_ref)


def join_kernel(first, second, third, *rest):
    out_ref = rest[-1]
    for i, ref in enumerate((first, second, third)):
        out_ref[i] = ref[...]


def one_hot(shape, row_of, column_of, dtype):
    row = lax.broadcasted_iota(jnp.int32, shape, 0)
    column = lax.broadcasted_iota(jnp.int32, shape, 1)
    return jnp.where(row_of(row) == column_of(column), 1.0, 0.0).astype(dtype)


def ladder_kernel(own_a, own_c, pairs_p, core_ref, *refs):
    core = core_ref[0]
    distance = (0, 1 + 2 * core, 2, 3 - 2 * core)
    lines, partners = refs[:SIDE], refs[SIDE : 2 * SIDE]
    ab_ref, ba_ref, out_ref, window, tile, total = refs[2 * SIDE :]
    wide = SIDE * own_c
    high = GROUP * own_a
    for j in range(WIN):
        rows = 0.0
        for s in range(SIDE):
            place = one_hot((wide, WIN * own_c), lambda r: r - distance[s] * own_c, lambda c: jnp.where((c >= j * own_c) & (c < (j + 1) * own_c), c - j * own_c, -wide - 1), jnp.bfloat16)
            rows += jnp.dot(place, partners[s][...], preferred_element_type=jnp.float32)
        window[j] = rows.astype(jnp.bfloat16)
    total[...] = jnp.zeros_like(total)
    for s in range(SIDE):
        for j in range(WIN):
            v = lax.dot_general(lines[s][...], window[j], ROWS_BY_ROWS, preferred_element_type=jnp.float32)
            tile[:, j] = v.astype(jnp.bfloat16).reshape(own_c // GROUP, high, wide)

        def one(g, carry):
            v = tile[g].reshape(WIN * high, wide)
            at = pl.ds(pl.multiple_of(g * GROUP * pairs_p, 16), GROUP * pairs_p)
            for i, amps in enumerate((ab_ref, ba_ref)):
                total[i] += lax.dot_general(v, amps[distance[s], at, :], ROWS_BY_ROWS, preferred_element_type=jnp.float32)
            return carry

        lax.fori_loop(0, own_c // GROUP, one, 0, unroll=True)
    shape = total.shape[1:]
    row = lax.broadcasted_iota(jnp.int32, shape, 0)
    column = lax.broadcasted_iota(jnp.int32, shape, 1)
    same = (row % high) // own_a == column // pairs_p
    fold = one_hot((own_a * WIN, shape[0]), lambda r: r, lambda c: (c % own_a) * WIN + c // high, jnp.float32)
    out = 0.0
    for i in range(2):
        to = one_hot((shape[1], LANES), lambda r: r % pairs_p + i * pairs_p, lambda c: c, jnp.float32)
        out += jnp.dot(jnp.where(same, total[i], 0.0), to, precision=HIGHEST, preferred_element_type=jnp.float32)
    out_ref[...] = jnp.dot(fold, out, precision=HIGHEST, preferred_element_type=jnp.float32)


def add_kernel(pairs_p, parts_ref, ab_ref, ba_ref):
    total = jnp.sum(parts_ref[...], axis=0)
    ab_ref[...] = total[:, :pairs_p]
    ba_ref[...] = pltpu.roll(total, LANES - pairs_p, 1)[:, :pairs_p]


def shards(df_blocks, amplitudes):
    own_a, own_c, aux = df_blocks.shape
    pairs_p, _, nv = amplitudes.shape
    bf16, f32 = jnp.bfloat16, jnp.float32
    vmem, smem, hbm = pl.BlockSpec(memory_space=pltpu.VMEM), pl.BlockSpec(memory_space=pltpu.SMEM), pl.BlockSpec(memory_space=pl.ANY)
    params = pltpu.CompilerParams(vmem_limit_bytes=48 * 1024 * 1024)
    rows, wide = own_c * pairs_p, SIDE * own_c
    place, core = lax.axis_index("col"), lax.axis_index("row") % 2
    at = jnp.stack([place % SIDE, place // SIDE, core]).astype(jnp.int32)

    partner = from_next_row(df_blocks[:WIN].reshape(WIN * own_c, aux))
    resident = jnp.transpose(df_blocks, (1, 0, 2)).reshape(own_c * own_a, aux)
    amps = jnp.transpose(amplitudes, (1, 0, 2)).reshape(rows, nv)
    sent, own = pl.pallas_call(
        functools.partial(pack_kernel, own_c),
        out_shape=(jax.ShapeDtypeStruct((3, rows + rows // CHUNKS, LANES), bf16), jax.ShapeDtypeStruct((2, rows, wide), bf16)),
        in_specs=[smem, vmem, hbm, hbm],
        out_specs=(vmem, vmem),
        compiler_params=params,
        name="pack",
    )(at, amps, partner, resident)
    lines = gathered(resident, 1, 0)
    mine = [core_0_along_x_core_1_along_y(sent[s - 1], s) for s in (1, 2, 3)]
    partners = gathered(partner, 0, 1)
    mine = pl.pallas_call(
        join_kernel,
        out_shape=jax.ShapeDtypeStruct(sent.shape, bf16),
        in_specs=[vmem] * 3 + [hbm] * 4,
        out_specs=vmem,
        compiler_params=params,
        name="join",
    )(*mine, lines[1], lines[3], partners[1], partners[3])
    other = between_cores(mine)
    ab, ba = pl.pallas_call(
        unpack_kernel,
        out_shape=(jax.ShapeDtypeStruct((SIDE, rows, wide), bf16),) * 2,
        in_specs=[smem, vmem, vmem, vmem],
        out_specs=(vmem, vmem),
        compiler_params=params,
        name="unpack",
    )(at[2:], own, mine, other)
    ba = jnp.transpose(ba.reshape(wide, pairs_p, wide), (2, 1, 0)).reshape(SIDE, rows, wide)
    part = pl.pallas_call(
        functools.partial(ladder_kernel, own_a, own_c, pairs_p),
        out_shape=jax.ShapeDtypeStruct((own_a * WIN, LANES), f32),
        in_specs=[smem] + [vmem] * (2 * SIDE + 2),
        out_specs=vmem,
        scratch_shapes=[
            pltpu.VMEM((WIN, wide, aux), bf16),
            pltpu.VMEM((own_c // GROUP, WIN, GROUP * own_a, wide), bf16),
            pltpu.VMEM((2, WIN * GROUP * own_a, GROUP * pairs_p), f32),
        ],
        compiler_params=params,
        name="ladders",
    )(at[2:], *lines, *partners, ab, ba)
    parts = lax.all_to_all(jnp.broadcast_to(part, (SIDE * SIDE, *part.shape)), "col", 0, 0, tiled=True)
    ab, ba = pl.pallas_call(
        functools.partial(add_kernel, pairs_p),
        out_shape=(jax.ShapeDtypeStruct((own_a * WIN, pairs_p), f32),) * 2,
        in_specs=[vmem],
        out_specs=(vmem, vmem),
        compiler_params=params,
        name="add",
    )(parts)
    return ab.reshape(own_a, WIN, pairs_p), ba.reshape(own_a, WIN, pairs_p)


def solution(mesh):
    in_specs = (P("row", "col", None), P(None, "col", None))
    out_specs = (P("row", None, None), P("row", None, None))
    return jax.shard_map(shards, mesh=mesh, in_specs=in_specs, out_specs=out_specs, check_vma=False)
```

```python
import functools

import jax
import jax.numpy as jnp
from jax import lax
from jax.experimental import pallas as pl
from jax.experimental.pallas import tpu as pltpu
from jax.sharding import PartitionSpec as P

WIN = 4
SIDE = 4
LANES = 128
CHUNKS = 6
GROUP = 4
HIGHEST = lax.Precision.HIGHEST
ROWS_BY_ROWS = (((1,), (1,)), ((), ()))


def moved(value, dx, dy):
    pairs = []
    for row in range(lax.axis_size("row")):
        sign = 1 - 2 * (row % 2)
        for yh in range(SIDE):
            for x in range(SIDE):
                to = (yh + sign * dy) % SIDE * SIDE + (x + sign * dx) % SIDE
                pairs.append(((row * SIDE + yh) * SIDE + x, row * SIDE * SIDE + to))
    return lax.ppermute(value, ("row", "col"), pairs)


def gathered(value, dx, dy):
    first = moved(value, dx, dy)
    return [value, first, moved(first, dx, dy), moved(value, -dx, -dy)]


def from_next_row(value):
    rows = lax.axis_size("row")
    return lax.ppermute(value, "row", [(source, (source - 1) % rows) for source in range(rows)])


def between_cores(value):
    rows = lax.axis_size("row")
    return lax.ppermute(value, "row", [(source, source ^ 1) for source in range(rows)])


def core_0_along_x_core_1_along_y(value, step):
    pairs = []
    for row in range(lax.axis_size("row")):
        for yh in range(SIDE):
            for x in range(SIDE):
                to = (yh, (x + step) % SIDE) if row % 2 == 0 else ((yh + step) % SIDE, x)
                pairs.append((row * SIDE * SIDE + yh * SIDE + x, row * SIDE * SIDE + to[0] * SIDE + to[1]))
    return lax.ppermute(value, ("row", "col"), pairs)


def pack_kernel(own_c, at_ref, amps_ref, sent_ref, own_ref):
    x, yh, core = at_ref[0], at_ref[1], at_ref[2]
    rows, nv = amps_ref.shape
    tail = SIDE * own_c - LANES
    part = rows // CHUNKS

    def source(n, kind, step):
        near, e = n // own_c, n % own_c
        ab = ((yh - near + SIDE) % SIDE) * SIDE + (x + step) % SIDE
        ba = ((yh + step) % SIDE) * SIDE + (x - near + SIDE) % SIDE
        return jnp.where(kind == 0, ab, ba) * own_c + e

    kinds = [(core, 1), (core, 2), (core, 3), (0, 0), (1, 0)]
    lane = lax.broadcasted_iota(jnp.int32, (1, LANES), 1)
    wanted = [source(lane, kind, step) for kind, step in kinds]
    ends = jnp.full((1, LANES), -1, jnp.int32)
    for i, (kind, step) in enumerate(kinds):
        here = (lane >= i * tail) & (lane < (i + 1) * tail)
        ends = jnp.where(here, source(lane - i * tail + LANES, kind, step), ends)
    wanted = jnp.concatenate(wanted + [ends], 1)
    chosen = lax.broadcasted_iota(jnp.int32, (nv, wanted.shape[1]), 0) == wanted
    chosen = jnp.where(chosen, 1.0, 0.0).astype(jnp.bfloat16)

    def one(k, carry):
        at = pl.multiple_of(k * part, 16)
        got = jnp.dot(amps_ref[pl.ds(at, part), :], chosen, preferred_element_type=jnp.float32)
        end = got[:, 5 * LANES :]
        for i in range(3):
            sent_ref[i, pl.ds(at, part), :] = got[:, i * LANES : (i + 1) * LANES].astype(jnp.bfloat16)
        for i in (3, 4):
            own_ref[i - 3, pl.ds(at, part), :LANES] = got[:, i * LANES : (i + 1) * LANES].astype(jnp.bfloat16)
            own_ref[i - 3, pl.ds(at, part), LANES:] = pltpu.roll(end, LANES - i * tail, 1)[:, :tail].astype(jnp.bfloat16)
        new = []
        for i in range(3):
            turned = pltpu.roll(end, (k * tail + LANES - i * tail) % LANES, 1)
            new.append(jnp.where((lane >= k * tail) & (lane < (k + 1) * tail), turned, carry[i]))
        return tuple(new)

    carry = tuple(jnp.zeros((part, LANES), jnp.float32) for _ in range(3))
    for k in range(CHUNKS):
        carry = one(k, carry)
    for i in range(3):
        sent_ref[i, rows:, :] = carry[i].astype(jnp.bfloat16)


def unpack_kernel(pairs_p, core_ref, own_ref, mine_ref, other_ref, ab_ref, ba_ref, main, end, turned_main, turned_end):
    core = core_ref[0]
    rows, wide = ab_ref.shape[1:]
    part = rows // CHUNKS
    tail = wide - LANES

    def put(ab_from, ba_from):
        for s in range(3):
            ab_ref[s + 1, :, :LANES] = ab_from[s, :rows, :]
            main[(s + 1) * rows : (s + 2) * rows, :] = ba_from[s, :rows, :].astype(jnp.float32)
            ab_end = ab_from[s, rows:, :].astype(jnp.float32)
            ba_end = ba_from[s, rows:, :].astype(jnp.float32)
            for k in range(CHUNKS):
                shift = (LANES - k * tail) % LANES
                at = k * part
                ab_ref[s + 1, at : at + part, LANES:] = pltpu.roll(ab_end, shift, 1)[:, :tail].astype(jnp.bfloat16)
                at += (s + 1) * rows
                end[at : at + part, :] = pltpu.roll(ba_end, shift, 1)

    ab_ref[0] = own_ref[0]
    main[:rows, :] = own_ref[1, :, :LANES].astype(jnp.float32)
    end[:rows, :tail] = own_ref[1, :, LANES:].astype(jnp.float32)

    @pl.when(core == 0)
    def _():
        put(mine_ref, other_ref)

    @pl.when(core == 1)
    def _():
        put(other_ref, mine_ref)

    def one(p, carry):
        body = jnp.concatenate([main[pl.ds(p, wide, stride=pairs_p), :].T, end[pl.ds(p, wide, stride=pairs_p), :].T[:tail]], 0)
        turned_main[pl.ds(p, wide, stride=pairs_p), :] = body[:, :LANES]
        turned_end[pl.ds(p, wide, stride=pairs_p), :tail] = body[:, LANES:]
        return carry

    lax.fori_loop(0, pairs_p, one, 0, unroll=4)
    for s in range(SIDE):
        ba_ref[s, :, :LANES] = turned_main[s * rows : (s + 1) * rows, :].astype(jnp.bfloat16)
        ba_ref[s, :, LANES:] = turned_end[s * rows : (s + 1) * rows, :tail].astype(jnp.bfloat16)


def join_kernel(first, second, third, *rest):
    out_ref = rest[-1]
    for i, ref in enumerate((first, second, third)):
        out_ref[i] = ref[...]


def one_hot(shape, row_of, column_of, dtype):
    row = lax.broadcasted_iota(jnp.int32, shape, 0)
    column = lax.broadcasted_iota(jnp.int32, shape, 1)
    return jnp.where(row_of(row) == column_of(column), 1.0, 0.0).astype(dtype)


def ladder_kernel(own_a, own_c, pairs_p, core_ref, *refs):
    core = core_ref[0]
    distance = (0, 1 + 2 * core, 2, 3 - 2 * core)
    lines, partners = refs[:SIDE], refs[SIDE : 2 * SIDE]
    ab_ref, ba_ref, out_ref, window, tile, total = refs[2 * SIDE :]
    wide = SIDE * own_c
    high = GROUP * own_a
    for j in range(WIN):
        rows = 0.0
        for s in range(SIDE):
            place = one_hot((wide, WIN * own_c), lambda r: r - distance[s] * own_c, lambda c: jnp.where((c >= j * own_c) & (c < (j + 1) * own_c), c - j * own_c, -wide - 1), jnp.bfloat16)
            rows += jnp.dot(place, partners[s][...], preferred_element_type=jnp.float32)
        window[j] = rows.astype(jnp.bfloat16)
    total[...] = jnp.zeros_like(total)
    for s in range(SIDE):
        for j in range(WIN):
            v = lax.dot_general(lines[s][...], window[j], ROWS_BY_ROWS, preferred_element_type=jnp.float32)
            tile[:, j] = v.astype(jnp.bfloat16).reshape(own_c // GROUP, high, wide)

        def one(g, carry):
            v = tile[g].reshape(WIN * high, wide)
            at = pl.ds(pl.multiple_of(g * GROUP * pairs_p, 16), GROUP * pairs_p)
            for i, amps in enumerate((ab_ref, ba_ref)):
                total[i] += lax.dot_general(v, amps[distance[s], at, :], ROWS_BY_ROWS, preferred_element_type=jnp.float32)
            return carry

        lax.fori_loop(0, own_c // GROUP, one, 0, unroll=True)
    shape = total.shape[1:]
    row = lax.broadcasted_iota(jnp.int32, shape, 0)
    column = lax.broadcasted_iota(jnp.int32, shape, 1)
    same = (row % high) // own_a == column // pairs_p
    fold = one_hot((own_a * WIN, shape[0]), lambda r: r, lambda c: (c % own_a) * WIN + c // high, jnp.float32)
    out = 0.0
    for i in range(2):
        to = one_hot((shape[1], LANES), lambda r: r % pairs_p + i * pairs_p, lambda c: c, jnp.float32)
        out += jnp.dot(jnp.where(same, total[i], 0.0), to, precision=HIGHEST, preferred_element_type=jnp.float32)
    out_ref[...] = jnp.dot(fold, out, precision=HIGHEST, preferred_element_type=jnp.float32)


def add_kernel(pairs_p, parts_ref, ab_ref, ba_ref):
    total = jnp.sum(parts_ref[...], axis=0)
    ab_ref[...] = total[:, :pairs_p]
    ba_ref[...] = pltpu.roll(total, LANES - pairs_p, 1)[:, :pairs_p]


def shards(df_blocks, amplitudes):
    own_a, own_c, aux = df_blocks.shape
    pairs_p, _, nv = amplitudes.shape
    bf16, f32 = jnp.bfloat16, jnp.float32
    vmem, smem, hbm = pl.BlockSpec(memory_space=pltpu.VMEM), pl.BlockSpec(memory_space=pltpu.SMEM), pl.BlockSpec(memory_space=pl.ANY)
    params = pltpu.CompilerParams(vmem_limit_bytes=48 * 1024 * 1024)
    rows, wide = own_c * pairs_p, SIDE * own_c
    place, core = lax.axis_index("col"), lax.axis_index("row") % 2
    at = jnp.stack([place % SIDE, place // SIDE, core]).astype(jnp.int32)

    partner = from_next_row(df_blocks[:WIN].reshape(WIN * own_c, aux))
    resident = jnp.transpose(df_blocks, (1, 0, 2)).reshape(own_c * own_a, aux)
    amps = jnp.transpose(amplitudes, (1, 0, 2)).reshape(rows, nv)
    sent, own = pl.pallas_call(
        functools.partial(pack_kernel, own_c),
        out_shape=(jax.ShapeDtypeStruct((3, rows + rows // CHUNKS, LANES), bf16), jax.ShapeDtypeStruct((2, rows, wide), bf16)),
        in_specs=[smem, vmem],
        out_specs=(vmem, vmem),
        compiler_params=params,
        name="pack",
    )(at, amps)
    lines = gathered(resident, 1, 0)
    mine = [core_0_along_x_core_1_along_y(sent[s - 1], s) for s in (1, 2, 3)]
    partners = gathered(partner, 0, 1)
    mine = pl.pallas_call(
        join_kernel,
        out_shape=jax.ShapeDtypeStruct(sent.shape, bf16),
        in_specs=[vmem] * 3 + [hbm] * 4,
        out_specs=vmem,
        compiler_params=params,
        name="join",
    )(*mine, lines[1], lines[3], partners[1], partners[3])
    other = between_cores(mine)
    ab, ba = pl.pallas_call(
        functools.partial(unpack_kernel, pairs_p),
        out_shape=(jax.ShapeDtypeStruct((SIDE, rows, wide), bf16),) * 2,
        in_specs=[smem, vmem, vmem, vmem],
        out_specs=(vmem, vmem),
        scratch_shapes=[pltpu.VMEM((SIDE * rows, LANES), f32)] * 4,
        compiler_params=params,
        name="unpack",
    )(at[2:], own, mine, other)
    part = pl.pallas_call(
        functools.partial(ladder_kernel, own_a, own_c, pairs_p),
        out_shape=jax.ShapeDtypeStruct((own_a * WIN, LANES), f32),
        in_specs=[smem] + [vmem] * (2 * SIDE + 2),
        out_specs=vmem,
        scratch_shapes=[
            pltpu.VMEM((WIN, wide, aux), bf16),
            pltpu.VMEM((own_c // GROUP, WIN, GROUP * own_a, wide), bf16),
            pltpu.VMEM((2, WIN * GROUP * own_a, GROUP * pairs_p), f32),
        ],
        compiler_params=params,
        name="ladders",
    )(at[2:], *lines, *partners, ab, ba)
    parts = lax.all_to_all(jnp.broadcast_to(part, (SIDE * SIDE, *part.shape)), "col", 0, 0, tiled=True)
    ab, ba = pl.pallas_call(
        functools.partial(add_kernel, pairs_p),
        out_shape=(jax.ShapeDtypeStruct((own_a * WIN, pairs_p), f32),) * 2,
        in_specs=[vmem],
        out_specs=(vmem, vmem),
        compiler_params=params,
        name="add",
    )(parts)
    return ab.reshape(own_a, WIN, pairs_p), ba.reshape(own_a, WIN, pairs_p)


def solution(mesh):
    in_specs = (P("row", "col", None), P(None, "col", None))
    out_specs = (P("row", None, None), P("row", None, None))
    return jax.shard_map(shards, mesh=mesh, in_specs=in_specs, out_specs=out_specs, check_vma=False)
```

```python
import functools

import jax
import jax.numpy as jnp
from jax import lax
from jax.experimental import pallas as pl
from jax.experimental.pallas import tpu as pltpu
from jax.sharding import PartitionSpec as P

WIN = 4
SIDE = 4
LANES = 128
CHUNKS = 6
GROUP = 4
HIGHEST = lax.Precision.HIGHEST
ROWS_BY_ROWS = (((1,), (1,)), ((), ()))


def moved(value, dx, dy, rows_on=0):
    pairs = []
    rows = lax.axis_size("row")
    for row in range(rows):
        sign = 1 - 2 * (row % 2)
        for yh in range(SIDE):
            for x in range(SIDE):
                to = (yh + sign * dy) % SIDE * SIDE + (x + sign * dx) % SIDE
                pairs.append((((row + rows_on) % rows * SIDE + yh) * SIDE + x, row * SIDE * SIDE + to))
    return lax.ppermute(value, ("row", "col"), pairs)


def gathered(value, dx, dy):
    first = moved(value, dx, dy)
    return [value, first, moved(first, dx, dy), moved(value, -dx, -dy)]


def between_cores(value):
    rows = lax.axis_size("row")
    return lax.ppermute(value, "row", [(source, source ^ 1) for source in range(rows)])


def core_0_along_x_core_1_along_y(value, step):
    pairs = []
    for row in range(lax.axis_size("row")):
        for yh in range(SIDE):
            for x in range(SIDE):
                to = (yh, (x + step) % SIDE) if row % 2 == 0 else ((yh + step) % SIDE, x)
                pairs.append((row * SIDE * SIDE + yh * SIDE + x, row * SIDE * SIDE + to[0] * SIDE + to[1]))
    return lax.ppermute(value, ("row", "col"), pairs)


def pack_kernel(own_c, at_ref, amps_ref, sent_ref, own_ref):
    x, yh, core = at_ref[0], at_ref[1], at_ref[2]
    rows, nv = amps_ref.shape
    tail = SIDE * own_c - LANES
    part = rows // CHUNKS

    def source(n, kind, step):
        near, e = n // own_c, n % own_c
        ab = ((yh - near + SIDE) % SIDE) * SIDE + (x + step) % SIDE
        ba = ((yh + step) % SIDE) * SIDE + (x - near + SIDE) % SIDE
        return jnp.where(kind == 0, ab, ba) * own_c + e

    kinds = [(core, 1), (core, 2), (core, 3), (0, 0), (1, 0)]
    lane = lax.broadcasted_iota(jnp.int32, (1, LANES), 1)
    wanted = [source(lane, kind, step) for kind, step in kinds]
    ends = jnp.full((1, LANES), -1, jnp.int32)
    for i, (kind, step) in enumerate(kinds):
        here = (lane >= i * tail) & (lane < (i + 1) * tail)
        ends = jnp.where(here, source(lane - i * tail + LANES, kind, step), ends)
    wanted = jnp.concatenate(wanted + [ends], 1)
    chosen = lax.broadcasted_iota(jnp.int32, (nv, wanted.shape[1]), 0) == wanted
    chosen = jnp.where(chosen, 1.0, 0.0).astype(jnp.bfloat16)

    def one(k, carry):
        at = pl.multiple_of(k * part, 16)
        got = jnp.dot(amps_ref[pl.ds(at, part), :], chosen, preferred_element_type=jnp.float32)
        end = got[:, 5 * LANES :]
        for i in range(3):
            sent_ref[i, pl.ds(at, part), :] = got[:, i * LANES : (i + 1) * LANES].astype(jnp.bfloat16)
        for i in (3, 4):
            own_ref[i - 3, pl.ds(at, part), :LANES] = got[:, i * LANES : (i + 1) * LANES].astype(jnp.bfloat16)
            own_ref[i - 3, pl.ds(at, part), LANES:] = pltpu.roll(end, LANES - i * tail, 1)[:, :tail].astype(jnp.bfloat16)
        new = []
        for i in range(3):
            turned = pltpu.roll(end, (k * tail + LANES - i * tail) % LANES, 1)
            new.append(jnp.where((lane >= k * tail) & (lane < (k + 1) * tail), turned, carry[i]))
        return tuple(new)

    carry = tuple(jnp.zeros((part, LANES), jnp.float32) for _ in range(3))
    for k in range(CHUNKS):
        carry = one(k, carry)
    for i in range(3):
        sent_ref[i, rows:, :] = carry[i].astype(jnp.bfloat16)


def unpack_kernel(pairs_p, core_ref, own_ref, mine_ref, other_ref, ab_ref, ba_ref, main, end, turned_main, turned_end):
    core = core_ref[0]
    rows, wide = ab_ref.shape[1:]
    part = rows // CHUNKS
    tail = wide - LANES

    def put(ab_from, ba_from):
        for s in range(3):
            ab_ref[s + 1, :, :LANES] = ab_from[s, :rows, :]
            main[(s + 1) * rows : (s + 2) * rows, :] = ba_from[s, :rows, :].astype(jnp.float32)
            ab_end = ab_from[s, rows:, :].astype(jnp.float32)
            ba_end = ba_from[s, rows:, :].astype(jnp.float32)
            for k in range(CHUNKS):
                shift = (LANES - k * tail) % LANES
                at = k * part
                ab_ref[s + 1, at : at + part, LANES:] = pltpu.roll(ab_end, shift, 1)[:, :tail].astype(jnp.bfloat16)
                at += (s + 1) * rows
                end[at : at + part, :] = pltpu.roll(ba_end, shift, 1)

    ab_ref[0] = own_ref[0]
    main[:rows, :] = own_ref[1, :, :LANES].astype(jnp.float32)
    end[:rows, :tail] = own_ref[1, :, LANES:].astype(jnp.float32)

    @pl.when(core == 0)
    def _():
        put(mine_ref, other_ref)

    @pl.when(core == 1)
    def _():
        put(other_ref, mine_ref)

    def one(p, carry):
        body = jnp.concatenate([main[pl.ds(p, wide, stride=pairs_p), :].T, end[pl.ds(p, wide, stride=pairs_p), :].T[:tail]], 0)
        turned_main[pl.ds(p, wide, stride=pairs_p), :] = body[:, :LANES]
        turned_end[pl.ds(p, wide, stride=pairs_p), :tail] = body[:, LANES:]
        return carry

    lax.fori_loop(0, pairs_p, one, 0, unroll=4)
    for s in range(SIDE):
        ba_ref[s, :, :LANES] = turned_main[s * rows : (s + 1) * rows, :].astype(jnp.bfloat16)
        ba_ref[s, :, LANES:] = turned_end[s * rows : (s + 1) * rows, :tail].astype(jnp.bfloat16)


def join_kernel(first, second, third, *rest):
    out_ref = rest[-1]
    for i, ref in enumerate((first, second, third)):
        out_ref[i] = ref[...]


def one_hot(shape, row_of, column_of, dtype):
    row = lax.broadcasted_iota(jnp.int32, shape, 0)
    column = lax.broadcasted_iota(jnp.int32, shape, 1)
    return jnp.where(row_of(row) == column_of(column), 1.0, 0.0).astype(dtype)


def ladder_kernel(own_a, own_c, pairs_p, core_ref, *refs):
    core = core_ref[0]
    distance = (0, 1 + 2 * core, 2, 3 - 2 * core)
    lines, partners = refs[:SIDE], refs[SIDE : 2 * SIDE]
    ab_ref, ba_ref, out_ref, window, tile, total = refs[2 * SIDE :]
    wide = SIDE * own_c
    high = GROUP * own_a
    for j in range(WIN):
        rows = 0.0
        for s in range(SIDE):
            place = one_hot((wide, WIN * own_c), lambda r: r - distance[s] * own_c, lambda c: jnp.where((c >= j * own_c) & (c < (j + 1) * own_c), c - j * own_c, -wide - 1), jnp.bfloat16)
            rows += jnp.dot(place, partners[s][...], preferred_element_type=jnp.float32)
        window[j] = rows.astype(jnp.bfloat16)
    total[...] = jnp.zeros_like(total)
    for s in range(SIDE):
        for j in range(WIN):
            v = lax.dot_general(lines[s][...], window[j], ROWS_BY_ROWS, preferred_element_type=jnp.float32)
            tile[:, j] = v.astype(jnp.bfloat16).reshape(own_c // GROUP, high, wide)

        def one(g, carry):
            v = tile[g].reshape(WIN * high, wide)
            at = pl.ds(pl.multiple_of(g * GROUP * pairs_p, 16), GROUP * pairs_p)
            for i, amps in enumerate((ab_ref, ba_ref)):
                total[i] += lax.dot_general(v, amps[distance[s], at, :], ROWS_BY_ROWS, preferred_element_type=jnp.float32)
            return carry

        lax.fori_loop(0, own_c // GROUP, one, 0, unroll=True)
    shape = total.shape[1:]
    row = lax.broadcasted_iota(jnp.int32, shape, 0)
    column = lax.broadcasted_iota(jnp.int32, shape, 1)
    same = (row % high) // own_a == column // pairs_p
    fold = one_hot((own_a * WIN, shape[0]), lambda r: r, lambda c: (c % own_a) * WIN + c // high, jnp.float32)
    out = 0.0
    for i in range(2):
        to = one_hot((shape[1], LANES), lambda r: r % pairs_p + i * pairs_p, lambda c: c, jnp.float32)
        out += jnp.dot(jnp.where(same, total[i], 0.0), to, precision=HIGHEST, preferred_element_type=jnp.float32)
    out_ref[...] = jnp.dot(fold, out, precision=HIGHEST, preferred_element_type=jnp.float32)


def add_kernel(pairs_p, parts_ref, ab_ref, ba_ref):
    total = jnp.sum(parts_ref[...], axis=0)
    ab_ref[...] = total[:, :pairs_p]
    ba_ref[...] = pltpu.roll(total, LANES - pairs_p, 1)[:, :pairs_p]


def shards(df_blocks, amplitudes):
    own_a, own_c, aux = df_blocks.shape
    pairs_p, _, nv = amplitudes.shape
    bf16, f32 = jnp.bfloat16, jnp.float32
    vmem, smem, hbm = pl.BlockSpec(memory_space=pltpu.VMEM), pl.BlockSpec(memory_space=pltpu.SMEM), pl.BlockSpec(memory_space=pl.ANY)
    params = pltpu.CompilerParams(vmem_limit_bytes=48 * 1024 * 1024)
    rows, wide = own_c * pairs_p, SIDE * own_c
    place, core = lax.axis_index("col"), lax.axis_index("row") % 2
    at = jnp.stack([place % SIDE, place // SIDE, core]).astype(jnp.int32)

    partner = df_blocks[:WIN].reshape(WIN * own_c, aux)
    resident = jnp.transpose(df_blocks, (1, 0, 2)).reshape(own_c * own_a, aux)
    amps = jnp.transpose(amplitudes, (1, 0, 2)).reshape(rows, nv)
    sent, own = pl.pallas_call(
        functools.partial(pack_kernel, own_c),
        out_shape=(jax.ShapeDtypeStruct((3, rows + rows // CHUNKS, LANES), bf16), jax.ShapeDtypeStruct((2, rows, wide), bf16)),
        in_specs=[smem, vmem],
        out_specs=(vmem, vmem),
        compiler_params=params,
        name="pack",
    )(at, amps)
    lines = gathered(resident, 1, 0)
    mine = [core_0_along_x_core_1_along_y(sent[s - 1], s) for s in (1, 2, 3)]
    first = moved(partner, 0, 1, 1)
    partners = [moved(partner, 0, 0, 1), first, moved(first, 0, 1), moved(partner, 0, -1, 1)]
    mine = pl.pallas_call(
        join_kernel,
        out_shape=jax.ShapeDtypeStruct(sent.shape, bf16),
        in_specs=[vmem] * 3 + [hbm] * 2,
        out_specs=vmem,
        compiler_params=params,
        name="join",
    )(*mine, lines[1], partners[1])
    other = between_cores(mine)
    ab, ba = pl.pallas_call(
        functools.partial(unpack_kernel, pairs_p),
        out_shape=(jax.ShapeDtypeStruct((SIDE, rows, wide), bf16),) * 2,
        in_specs=[smem, vmem, vmem, vmem],
        out_specs=(vmem, vmem),
        scratch_shapes=[pltpu.VMEM((SIDE * rows, LANES), f32)] * 4,
        compiler_params=params,
        name="unpack",
    )(at[2:], own, mine, other)
    part = pl.pallas_call(
        functools.partial(ladder_kernel, own_a, own_c, pairs_p),
        out_shape=jax.ShapeDtypeStruct((own_a * WIN, LANES), f32),
        in_specs=[smem] + [vmem] * (2 * SIDE + 2),
        out_specs=vmem,
        scratch_shapes=[
            pltpu.VMEM((WIN, wide, aux), bf16),
            pltpu.VMEM((own_c // GROUP, WIN, GROUP * own_a, wide), bf16),
            pltpu.VMEM((2, WIN * GROUP * own_a, GROUP * pairs_p), f32),
        ],
        compiler_params=params,
        name="ladders",
    )(at[2:], *lines, *partners, ab, ba)
    parts = lax.all_to_all(jnp.broadcast_to(part, (SIDE * SIDE, *part.shape)), "col", 0, 0, tiled=True)
    ab, ba = pl.pallas_call(
        functools.partial(add_kernel, pairs_p),
        out_shape=(jax.ShapeDtypeStruct((own_a * WIN, pairs_p), f32),) * 2,
        in_specs=[vmem],
        out_specs=(vmem, vmem),
        compiler_params=params,
        name="add",
    )(parts)
    return ab.reshape(own_a, WIN, pairs_p), ba.reshape(own_a, WIN, pairs_p)


def solution(mesh):
    in_specs = (P("row", "col", None), P(None, "col", None))
    out_specs = (P("row", None, None), P("row", None, None))
    return jax.shard_map(shards, mesh=mesh, in_specs=in_specs, out_specs=out_specs, check_vma=False)
```

```python
import functools

import jax
import jax.numpy as jnp
from jax import lax
from jax.experimental import pallas as pl
from jax.experimental.pallas import tpu as pltpu
from jax.sharding import PartitionSpec as P

WIN = 4
SIDE = 4
LANES = 128
CHUNKS = 6
GROUP = 4
HIGHEST = lax.Precision.HIGHEST
ROWS_BY_ROWS = (((1,), (1,)), ((), ()))


def moved(value, dx, dy):
    pairs = []
    for row in range(lax.axis_size("row")):
        sign = 1 - 2 * (row % 2)
        for yh in range(SIDE):
            for x in range(SIDE):
                to = (yh + sign * dy) % SIDE * SIDE + (x + sign * dx) % SIDE
                pairs.append(((row * SIDE + yh) * SIDE + x, row * SIDE * SIDE + to))
    return lax.ppermute(value, ("row", "col"), pairs)


def gathered(value, dx, dy):
    first = moved(value, dx, dy)
    return [value, first, moved(first, dx, dy), moved(value, -dx, -dy)]


def from_next_row(value):
    rows = lax.axis_size("row")
    return lax.ppermute(value, "row", [(source, (source - 1) % rows) for source in range(rows)])


def between_cores(value):
    rows = lax.axis_size("row")
    return lax.ppermute(value, "row", [(source, source ^ 1) for source in range(rows)])


def core_0_along_x_core_1_along_y(value, step):
    pairs = []
    for row in range(lax.axis_size("row")):
        for yh in range(SIDE):
            for x in range(SIDE):
                to = (yh, (x + step) % SIDE) if row % 2 == 0 else ((yh + step) % SIDE, x)
                pairs.append((row * SIDE * SIDE + yh * SIDE + x, row * SIDE * SIDE + to[0] * SIDE + to[1]))
    return lax.ppermute(value, ("row", "col"), pairs)


def pack_kernel(own_c, at_ref, amps_ref, sent_ref, own_ref):
    x, yh, core = at_ref[0], at_ref[1], at_ref[2]
    rows, nv = amps_ref.shape
    tail = SIDE * own_c - LANES
    part = rows // CHUNKS

    def source(n, kind, step):
        near, e = n // own_c, n % own_c
        ab = ((yh - near + SIDE) % SIDE) * SIDE + (x + step) % SIDE
        ba = ((yh + step) % SIDE) * SIDE + (x - near + SIDE) % SIDE
        return jnp.where(kind == 0, ab, ba) * own_c + e

    kinds = [(core, 1), (core, 2), (core, 3), (0, 0), (1, 0)]
    lane = lax.broadcasted_iota(jnp.int32, (1, LANES), 1)
    wanted = [source(lane, kind, step) for kind, step in kinds]
    ends = jnp.full((1, LANES), -1, jnp.int32)
    for i, (kind, step) in enumerate(kinds):
        here = (lane >= i * tail) & (lane < (i + 1) * tail)
        ends = jnp.where(here, source(lane - i * tail + LANES, kind, step), ends)
    wanted = jnp.concatenate(wanted + [ends], 1)
    chosen = lax.broadcasted_iota(jnp.int32, (nv, wanted.shape[1]), 0) == wanted
    chosen = jnp.where(chosen, 1.0, 0.0).astype(jnp.bfloat16)

    def one(k, carry):
        at = pl.multiple_of(k * part, 16)
        got = jnp.dot(amps_ref[pl.ds(at, part), :], chosen, preferred_element_type=jnp.float32)
        end = got[:, 5 * LANES :]
        for i in range(3):
            sent_ref[i, pl.ds(at, part), :] = got[:, i * LANES : (i + 1) * LANES].astype(jnp.bfloat16)
        for i in (3, 4):
            own_ref[i - 3, pl.ds(at, part), :LANES] = got[:, i * LANES : (i + 1) * LANES].astype(jnp.bfloat16)
            own_ref[i - 3, pl.ds(at, part), LANES:] = pltpu.roll(end, LANES - i * tail, 1)[:, :tail].astype(jnp.bfloat16)
        new = []
        for i in range(3):
            turned = pltpu.roll(end, (k * tail + LANES - i * tail) % LANES, 1)
            new.append(jnp.where((lane >= k * tail) & (lane < (k + 1) * tail), turned, carry[i]))
        return tuple(new)

    carry = tuple(jnp.zeros((part, LANES), jnp.float32) for _ in range(3))
    for k in range(CHUNKS):
        carry = one(k, carry)
    for i in range(3):
        sent_ref[i, rows:, :] = carry[i].astype(jnp.bfloat16)


def unpack_kernel(pairs_p, core_ref, own_ref, mine_ref, other_ref, ab_ref, ba_ref, main, end, turned_main, turned_end):
    core = core_ref[0]
    rows, wide = ab_ref.shape[1:]
    part = rows // CHUNKS
    tail = wide - LANES

    def put(ab_from, ba_from):
        for s in range(3):
            ab_ref[s + 1, :, :LANES] = ab_from[s, :rows, :]
            main[(s + 1) * rows : (s + 2) * rows, :] = ba_from[s, :rows, :].astype(jnp.float32)
            ab_end = ab_from[s, rows:, :].astype(jnp.float32)
            ba_end = ba_from[s, rows:, :].astype(jnp.float32)
            for k in range(CHUNKS):
                shift = (LANES - k * tail) % LANES
                at = k * part
                ab_ref[s + 1, at : at + part, LANES:] = pltpu.roll(ab_end, shift, 1)[:, :tail].astype(jnp.bfloat16)
                at += (s + 1) * rows
                end[at : at + part, :] = pltpu.roll(ba_end, shift, 1)

    ab_ref[0] = own_ref[0]
    main[:rows, :] = own_ref[1, :, :LANES].astype(jnp.float32)
    end[:rows, :tail] = own_ref[1, :, LANES:].astype(jnp.float32)

    @pl.when(core == 0)
    def _():
        put(mine_ref, other_ref)

    @pl.when(core == 1)
    def _():
        put(other_ref, mine_ref)

    def one(p, carry):
        body = jnp.concatenate([main[pl.ds(p, wide, stride=pairs_p), :].T, end[pl.ds(p, wide, stride=pairs_p), :].T[:tail]], 0)
        turned_main[pl.ds(p, wide, stride=pairs_p), :] = body[:, :LANES]
        turned_end[pl.ds(p, wide, stride=pairs_p), :tail] = body[:, LANES:]
        return carry

    lax.fori_loop(0, pairs_p, one, 0, unroll=16)
    for s in range(SIDE):
        ba_ref[s, :, :LANES] = turned_main[s * rows : (s + 1) * rows, :].astype(jnp.bfloat16)
        ba_ref[s, :, LANES:] = turned_end[s * rows : (s + 1) * rows, :tail].astype(jnp.bfloat16)


def join_kernel(first, second, third, *rest):
    out_ref = rest[-1]
    for i, ref in enumerate((first, second, third)):
        out_ref[i] = ref[...]


def one_hot(shape, row_of, column_of, dtype):
    row = lax.broadcasted_iota(jnp.int32, shape, 0)
    column = lax.broadcasted_iota(jnp.int32, shape, 1)
    return jnp.where(row_of(row) == column_of(column), 1.0, 0.0).astype(dtype)


def ladder_kernel(own_a, own_c, pairs_p, core_ref, *refs):
    core = core_ref[0]
    distance = (0, 1 + 2 * core, 2, 3 - 2 * core)
    lines, partners = refs[:SIDE], refs[SIDE : 2 * SIDE]
    ab_ref, ba_ref, out_ref, window, tile, total = refs[2 * SIDE :]
    wide = SIDE * own_c
    high = GROUP * own_a
    shape = (wide, SIDE * WIN * own_c)
    row = lax.broadcasted_iota(jnp.int32, shape, 0)
    column = lax.broadcasted_iota(jnp.int32, shape, 1)
    arrived = column // (WIN * own_c)
    far = jnp.where(arrived == 1, distance[1], jnp.where(arrived == 3, distance[3], arrived))
    kept = (column % own_c + far * own_c) == row
    held = jnp.concatenate([partner[...] for partner in partners], 0)
    every = jnp.concatenate([line[...] for line in lines], 0)
    for j in range(WIN):
        place = jnp.where(kept & (column // own_c % WIN == j), 1.0, 0.0).astype(jnp.bfloat16)
        window[...] = jnp.dot(place, held, preferred_element_type=jnp.float32).astype(jnp.bfloat16)
        v = lax.dot_general(every, window[...], ROWS_BY_ROWS, preferred_element_type=jnp.float32)
        tile[:, j] = v.astype(jnp.bfloat16).reshape(SIDE * own_c // GROUP, high, wide)
    total[...] = jnp.zeros_like(total)
    groups = own_c // GROUP
    for s in range(SIDE):
        for i, amps in enumerate((ab_ref, ba_ref)):
            more = total[i]
            for g in range(groups):
                v = tile[s * groups + g].reshape(WIN * high, wide)
                part = amps[distance[s], g * GROUP * pairs_p : (g + 1) * GROUP * pairs_p, :]
                more += lax.dot_general(v, part, ROWS_BY_ROWS, preferred_element_type=jnp.float32)
            total[i] = more
    shape = total.shape[1:]
    row = lax.broadcasted_iota(jnp.int32, shape, 0)
    column = lax.broadcasted_iota(jnp.int32, shape, 1)
    same = (row % high) // own_a == column // pairs_p
    fold = one_hot((own_a * WIN, shape[0]), lambda r: r, lambda c: (c % own_a) * WIN + c // high, jnp.float32)
    out = 0.0
    for i in range(2):
        to = one_hot((shape[1], LANES), lambda r: r % pairs_p + i * pairs_p, lambda c: c, jnp.float32)
        out += jnp.dot(jnp.where(same, total[i], 0.0), to, precision=HIGHEST, preferred_element_type=jnp.float32)
    out_ref[...] = jnp.dot(fold, out, precision=HIGHEST, preferred_element_type=jnp.float32)


def add_kernel(pairs_p, parts_ref, ab_ref, ba_ref):
    total = jnp.sum(parts_ref[...], axis=0)
    ab_ref[...] = total[:, :pairs_p]
    ba_ref[...] = pltpu.roll(total, LANES - pairs_p, 1)[:, :pairs_p]


def shards(df_blocks, amplitudes):
    own_a, own_c, aux = df_blocks.shape
    pairs_p, _, nv = amplitudes.shape
    bf16, f32 = jnp.bfloat16, jnp.float32
    vmem, smem, hbm = pl.BlockSpec(memory_space=pltpu.VMEM), pl.BlockSpec(memory_space=pltpu.SMEM), pl.BlockSpec(memory_space=pl.ANY)
    params = pltpu.CompilerParams(vmem_limit_bytes=48 * 1024 * 1024)
    rows, wide = own_c * pairs_p, SIDE * own_c
    place, core = lax.axis_index("col"), lax.axis_index("row") % 2
    at = jnp.stack([place % SIDE, place // SIDE, core]).astype(jnp.int32)

    partner = from_next_row(df_blocks[:WIN].reshape(WIN * own_c, aux))
    resident = jnp.transpose(df_blocks, (1, 0, 2)).reshape(own_c * own_a, aux)
    amps = jnp.transpose(amplitudes, (1, 0, 2)).reshape(rows, nv)
    sent, own = pl.pallas_call(
        functools.partial(pack_kernel, own_c),
        out_shape=(jax.ShapeDtypeStruct((3, rows + rows // CHUNKS, LANES), bf16), jax.ShapeDtypeStruct((2, rows, wide), bf16)),
        in_specs=[smem, vmem],
        out_specs=(vmem, vmem),
        compiler_params=params,
        name="pack",
    )(at, amps)
    lines = gathered(resident, 1, 0)
    mine = [core_0_along_x_core_1_along_y(sent[s - 1], s) for s in (1, 2, 3)]
    partners = gathered(partner, 0, 1)
    mine = pl.pallas_call(
        join_kernel,
        out_shape=jax.ShapeDtypeStruct(sent.shape, bf16),
        in_specs=[vmem] * 3 + [hbm] * 3,
        out_specs=vmem,
        compiler_params=params,
        name="join",
    )(*mine, lines[1], lines[3], partners[1])
    other = between_cores(mine)
    ab, ba = pl.pallas_call(
        functools.partial(unpack_kernel, pairs_p),
        out_shape=(jax.ShapeDtypeStruct((SIDE, rows, wide), bf16),) * 2,
        in_specs=[smem, vmem, vmem, vmem],
        out_specs=(vmem, vmem),
        scratch_shapes=[pltpu.VMEM((SIDE * rows, LANES), f32)] * 4,
        compiler_params=params,
        name="unpack",
    )(at[2:], own, mine, other)
    part = pl.pallas_call(
        functools.partial(ladder_kernel, own_a, own_c, pairs_p),
        out_shape=jax.ShapeDtypeStruct((own_a * WIN, LANES), f32),
        in_specs=[smem] + [vmem] * (2 * SIDE + 2),
        out_specs=vmem,
        scratch_shapes=[
            pltpu.VMEM((wide, aux), bf16),
            pltpu.VMEM((wide // GROUP, WIN, GROUP * own_a, wide), bf16),
            pltpu.VMEM((2, WIN * GROUP * own_a, GROUP * pairs_p), f32),
        ],
        compiler_params=params,
        name="ladders",
    )(at[2:], *lines, *partners, ab, ba)
    parts = lax.all_to_all(jnp.broadcast_to(part, (SIDE * SIDE, *part.shape)), "col", 0, 0, tiled=True)
    ab, ba = pl.pallas_call(
        functools.partial(add_kernel, pairs_p),
        out_shape=(jax.ShapeDtypeStruct((own_a * WIN, pairs_p), f32),) * 2,
        in_specs=[vmem],
        out_specs=(vmem, vmem),
        compiler_params=params,
        name="add",
    )(parts)
    return ab.reshape(own_a, WIN, pairs_p), ba.reshape(own_a, WIN, pairs_p)


def solution(mesh):
    in_specs = (P("row", "col", None), P(None, "col", None))
    out_specs = (P("row", None, None), P("row", None, None))
    return jax.shard_map(shards, mesh=mesh, in_specs=in_specs, out_specs=out_specs, check_vma=False)
```

```python
import functools

import jax
import jax.numpy as jnp
from jax import lax
from jax.experimental import pallas as pl
from jax.experimental.pallas import tpu as pltpu
from jax.sharding import PartitionSpec as P

WIN = 4
SIDE = 4
LANES = 128
CHUNKS = 6
GROUP = 4
HIGHEST = lax.Precision.HIGHEST
ROWS_BY_ROWS = (((1,), (1,)), ((), ()))


def moved(value, dx, dy):
    pairs = []
    for row in range(lax.axis_size("row")):
        sign = 1 - 2 * (row % 2)
        for yh in range(SIDE):
            for x in range(SIDE):
                to = (yh + sign * dy) % SIDE * SIDE + (x + sign * dx) % SIDE
                pairs.append(((row * SIDE + yh) * SIDE + x, row * SIDE * SIDE + to))
    return lax.ppermute(value, ("row", "col"), pairs)


def gathered(value, dx, dy):
    first = moved(value, dx, dy)
    return [value, first, moved(first, dx, dy), moved(value, -dx, -dy)]


def from_next_row(value):
    rows = lax.axis_size("row")
    return lax.ppermute(value, "row", [(source, (source - 1) % rows) for source in range(rows)])


def between_cores(value):
    rows = lax.axis_size("row")
    return lax.ppermute(value, "row", [(source, source ^ 1) for source in range(rows)])


def core_0_along_x_core_1_along_y(value, step):
    pairs = []
    for row in range(lax.axis_size("row")):
        for yh in range(SIDE):
            for x in range(SIDE):
                to = (yh, (x + step) % SIDE) if row % 2 == 0 else ((yh + step) % SIDE, x)
                pairs.append((row * SIDE * SIDE + yh * SIDE + x, row * SIDE * SIDE + to[0] * SIDE + to[1]))
    return lax.ppermute(value, ("row", "col"), pairs)


def pack_kernel(own_c, at_ref, amps_ref, sent_ref, own_ref):
    x, yh, core = at_ref[0], at_ref[1], at_ref[2]
    rows, nv = amps_ref.shape
    tail = SIDE * own_c - LANES
    part = rows // CHUNKS

    def source(n, kind, step):
        near, e = n // own_c, n % own_c
        ab = ((yh - near + SIDE) % SIDE) * SIDE + (x + step) % SIDE
        ba = ((yh + step) % SIDE) * SIDE + (x - near + SIDE) % SIDE
        return jnp.where(kind == 0, ab, ba) * own_c + e

    kinds = [(core, 1), (core, 2), (core, 3), (0, 0), (1, 0)]
    lane = lax.broadcasted_iota(jnp.int32, (1, LANES), 1)
    wanted = [source(lane, kind, step) for kind, step in kinds]
    ends = jnp.full((1, LANES), -1, jnp.int32)
    for i, (kind, step) in enumerate(kinds):
        here = (lane >= i * tail) & (lane < (i + 1) * tail)
        ends = jnp.where(here, source(lane - i * tail + LANES, kind, step), ends)
    wanted = jnp.concatenate(wanted + [ends], 1)
    chosen = lax.broadcasted_iota(jnp.int32, (nv, wanted.shape[1]), 0) == wanted
    chosen = jnp.where(chosen, 1.0, 0.0).astype(jnp.bfloat16)

    def one(k, carry):
        at = pl.multiple_of(k * part, 16)
        got = jnp.dot(amps_ref[pl.ds(at, part), :], chosen, preferred_element_type=jnp.float32)
        end = got[:, 5 * LANES :]
        for i in range(3):
            sent_ref[i, pl.ds(at, part), :] = got[:, i * LANES : (i + 1) * LANES].astype(jnp.bfloat16)
        for i in (3, 4):
            own_ref[i - 3, pl.ds(at, part), :LANES] = got[:, i * LANES : (i + 1) * LANES].astype(jnp.bfloat16)
            own_ref[i - 3, pl.ds(at, part), LANES:] = pltpu.roll(end, LANES - i * tail, 1)[:, :tail].astype(jnp.bfloat16)
        new = []
        for i in range(3):
            turned = pltpu.roll(end, (k * tail + LANES - i * tail) % LANES, 1)
            new.append(jnp.where((lane >= k * tail) & (lane < (k + 1) * tail), turned, carry[i]))
        return tuple(new)

    carry = tuple(jnp.zeros((part, LANES), jnp.float32) for _ in range(3))
    for k in range(CHUNKS):
        carry = one(k, carry)
    for i in range(3):
        sent_ref[i, rows:, :] = carry[i].astype(jnp.bfloat16)


def unpack_kernel(pairs_p, core_ref, own_ref, mine_ref, other_ref, *refs):
    ab_ref, ba_ref, main, end, turned_main, turned_end = refs[-6:]
    core = core_ref[0]
    rows, wide = ab_ref.shape[1:]
    part = rows // CHUNKS
    tail = wide - LANES

    def put(ab_from, ba_from):
        for s in range(3):
            ab_ref[s + 1, :, :LANES] = ab_from[s, :rows, :]
            main[(s + 1) * rows : (s + 2) * rows, :] = ba_from[s, :rows, :].astype(jnp.float32)
            ab_end = ab_from[s, rows:, :].astype(jnp.float32)
            ba_end = ba_from[s, rows:, :].astype(jnp.float32)
            for k in range(CHUNKS):
                shift = (LANES - k * tail) % LANES
                at = k * part
                ab_ref[s + 1, at : at + part, LANES:] = pltpu.roll(ab_end, shift, 1)[:, :tail].astype(jnp.bfloat16)
                at += (s + 1) * rows
                end[at : at + part, :] = pltpu.roll(ba_end, shift, 1)

    ab_ref[0] = own_ref[0]
    main[:rows, :] = own_ref[1, :, :LANES].astype(jnp.float32)
    end[:rows, :tail] = own_ref[1, :, LANES:].astype(jnp.float32)

    @pl.when(core == 0)
    def _():
        put(mine_ref, other_ref)

    @pl.when(core == 1)
    def _():
        put(other_ref, mine_ref)

    def one(p, carry):
        body = jnp.concatenate([main[pl.ds(p, wide, stride=pairs_p), :].T, end[pl.ds(p, wide, stride=pairs_p), :].T[:tail]], 0)
        turned_main[pl.ds(p, wide, stride=pairs_p), :] = body[:, :LANES]
        turned_end[pl.ds(p, wide, stride=pairs_p), :tail] = body[:, LANES:]
        return carry

    lax.fori_loop(0, pairs_p, one, 0, unroll=16)
    for s in range(SIDE):
        ba_ref[s, :, :LANES] = turned_main[s * rows : (s + 1) * rows, :].astype(jnp.bfloat16)
        ba_ref[s, :, LANES:] = turned_end[s * rows : (s + 1) * rows, :tail].astype(jnp.bfloat16)


def join_kernel(first, second, third, *rest):
    out_ref = rest[-1]
    for i, ref in enumerate((first, second, third)):
        out_ref[i] = ref[...]


def one_hot(shape, row_of, column_of, dtype):
    row = lax.broadcasted_iota(jnp.int32, shape, 0)
    column = lax.broadcasted_iota(jnp.int32, shape, 1)
    return jnp.where(row_of(row) == column_of(column), 1.0, 0.0).astype(dtype)


def ladder_kernel(own_a, own_c, pairs_p, core_ref, *refs):
    core = core_ref[0]
    distance = (0, 1 + 2 * core, 2, 3 - 2 * core)
    lines, partners = refs[:SIDE], refs[SIDE : 2 * SIDE]
    ab_ref, ba_ref, out_ref, window, tile, total = refs[2 * SIDE :]
    wide = SIDE * own_c
    high = GROUP * own_a
    shape = (wide, SIDE * WIN * own_c)
    row = lax.broadcasted_iota(jnp.int32, shape, 0)
    column = lax.broadcasted_iota(jnp.int32, shape, 1)
    arrived = column // (WIN * own_c)
    far = jnp.where(arrived == 1, distance[1], jnp.where(arrived == 3, distance[3], arrived))
    kept = (column % own_c + far * own_c) == row
    held = jnp.concatenate([partner[...] for partner in partners], 0)
    every = jnp.concatenate([line[...] for line in lines], 0)
    for j in range(WIN):
        place = jnp.where(kept & (column // own_c % WIN == j), 1.0, 0.0).astype(jnp.bfloat16)
        window[...] = jnp.dot(place, held, preferred_element_type=jnp.float32).astype(jnp.bfloat16)
        v = lax.dot_general(every, window[...], ROWS_BY_ROWS, preferred_element_type=jnp.float32)
        tile[:, j] = v.astype(jnp.bfloat16).reshape(SIDE * own_c // GROUP, high, wide)
    total[...] = jnp.zeros_like(total)
    groups = own_c // GROUP
    for s in range(SIDE):
        for i, amps in enumerate((ab_ref, ba_ref)):
            more = total[i]
            for g in range(groups):
                v = tile[s * groups + g].reshape(WIN * high, wide)
                part = amps[distance[s], g * GROUP * pairs_p : (g + 1) * GROUP * pairs_p, :]
                more += lax.dot_general(v, part, ROWS_BY_ROWS, preferred_element_type=jnp.float32)
            total[i] = more
    shape = total.shape[1:]
    row = lax.broadcasted_iota(jnp.int32, shape, 0)
    column = lax.broadcasted_iota(jnp.int32, shape, 1)
    same = (row % high) // own_a == column // pairs_p
    fold = one_hot((own_a * WIN, shape[0]), lambda r: r, lambda c: (c % own_a) * WIN + c // high, jnp.float32)
    out = 0.0
    for i in range(2):
        to = one_hot((shape[1], LANES), lambda r: r % pairs_p + i * pairs_p, lambda c: c, jnp.float32)
        out += jnp.dot(jnp.where(same, total[i], 0.0), to, precision=HIGHEST, preferred_element_type=jnp.float32)
    out_ref[...] = jnp.dot(fold, out, precision=HIGHEST, preferred_element_type=jnp.float32)


def add_kernel(pairs_p, parts_ref, ab_ref, ba_ref):
    total = jnp.sum(parts_ref[...], axis=0)
    ab_ref[...] = total[:, :pairs_p]
    ba_ref[...] = pltpu.roll(total, LANES - pairs_p, 1)[:, :pairs_p]


def shards(df_blocks, amplitudes):
    own_a, own_c, aux = df_blocks.shape
    pairs_p, _, nv = amplitudes.shape
    bf16, f32 = jnp.bfloat16, jnp.float32
    vmem, smem, hbm = pl.BlockSpec(memory_space=pltpu.VMEM), pl.BlockSpec(memory_space=pltpu.SMEM), pl.BlockSpec(memory_space=pl.ANY)
    params = pltpu.CompilerParams(vmem_limit_bytes=48 * 1024 * 1024)
    rows, wide = own_c * pairs_p, SIDE * own_c
    place, core = lax.axis_index("col"), lax.axis_index("row") % 2
    at = jnp.stack([place % SIDE, place // SIDE, core]).astype(jnp.int32)

    partner = from_next_row(df_blocks[:WIN].reshape(WIN * own_c, aux))
    resident = jnp.transpose(df_blocks, (1, 0, 2)).reshape(own_c * own_a, aux)
    amps = jnp.transpose(amplitudes, (1, 0, 2)).reshape(rows, nv)
    sent, own = pl.pallas_call(
        functools.partial(pack_kernel, own_c),
        out_shape=(jax.ShapeDtypeStruct((3, rows + rows // CHUNKS, LANES), bf16), jax.ShapeDtypeStruct((2, rows, wide), bf16)),
        in_specs=[smem, vmem],
        out_specs=(vmem, vmem),
        compiler_params=params,
        name="pack",
    )(at, amps)
    lines = gathered(resident, 1, 0)
    mine = [core_0_along_x_core_1_along_y(sent[s - 1], s) for s in (1, 2, 3)]
    partners = gathered(partner, 0, 1)
    mine = pl.pallas_call(
        join_kernel,
        out_shape=jax.ShapeDtypeStruct(sent.shape, bf16),
        in_specs=[vmem] * 3 + [hbm] * 2,
        out_specs=vmem,
        compiler_params=params,
        name="join",
    )(*mine, lines[1], partners[0])
    other = between_cores(mine)
    ab, ba = pl.pallas_call(
        functools.partial(unpack_kernel, pairs_p),
        out_shape=(jax.ShapeDtypeStruct((SIDE, rows, wide), bf16),) * 2,
        in_specs=[smem, vmem, vmem, vmem] + [hbm] * 1,
        out_specs=(vmem, vmem),
        scratch_shapes=[pltpu.VMEM((SIDE * rows, LANES), f32)] * 4,
        compiler_params=params,
        name="unpack",
    )(at[2:], own, mine, other, partners[1])
    part = pl.pallas_call(
        functools.partial(ladder_kernel, own_a, own_c, pairs_p),
        out_shape=jax.ShapeDtypeStruct((own_a * WIN, LANES), f32),
        in_specs=[smem] + [vmem] * (2 * SIDE + 2),
        out_specs=vmem,
        scratch_shapes=[
            pltpu.VMEM((wide, aux), bf16),
            pltpu.VMEM((wide // GROUP, WIN, GROUP * own_a, wide), bf16),
            pltpu.VMEM((2, WIN * GROUP * own_a, GROUP * pairs_p), f32),
        ],
        compiler_params=params,
        name="ladders",
    )(at[2:], *lines, *partners, ab, ba)
    parts = lax.all_to_all(jnp.broadcast_to(part, (SIDE * SIDE, *part.shape)), "col", 0, 0, tiled=True)
    ab, ba = pl.pallas_call(
        functools.partial(add_kernel, pairs_p),
        out_shape=(jax.ShapeDtypeStruct((own_a * WIN, pairs_p), f32),) * 2,
        in_specs=[vmem],
        out_specs=(vmem, vmem),
        compiler_params=params,
        name="add",
    )(parts)
    return ab.reshape(own_a, WIN, pairs_p), ba.reshape(own_a, WIN, pairs_p)


def solution(mesh):
    in_specs = (P("row", "col", None), P(None, "col", None))
    out_specs = (P("row", None, None), P("row", None, None))
    return jax.shard_map(shards, mesh=mesh, in_specs=in_specs, out_specs=out_specs, check_vma=False)
```

```python
import functools

import jax
import jax.numpy as jnp
from jax import lax
from jax.experimental import pallas as pl
from jax.experimental.pallas import tpu as pltpu
from jax.sharding import PartitionSpec as P

WIN = 4
SIDE = 4
LANES = 128
CHUNKS = 6
GROUP = 4
HIGHEST = lax.Precision.HIGHEST
ROWS_BY_ROWS = (((1,), (1,)), ((), ()))


def moved(value, dx, dy):
    pairs = []
    for row in range(lax.axis_size("row")):
        sign = 1 - 2 * (row % 2)
        for yh in range(SIDE):
            for x in range(SIDE):
                to = (yh + sign * dy) % SIDE * SIDE + (x + sign * dx) % SIDE
                pairs.append(((row * SIDE + yh) * SIDE + x, row * SIDE * SIDE + to))
    return lax.ppermute(value, ("row", "col"), pairs)


def gathered(value, dx, dy):
    first = moved(value, dx, dy)
    return [value, first, moved(first, dx, dy), moved(value, -dx, -dy)]


def from_next_row(value):
    rows = lax.axis_size("row")
    return lax.ppermute(value, "row", [(source, (source - 1) % rows) for source in range(rows)])


def between_cores(value):
    rows = lax.axis_size("row")
    return lax.ppermute(value, "row", [(source, source ^ 1) for source in range(rows)])


def core_0_along_x_core_1_along_y(value, step):
    pairs = []
    for row in range(lax.axis_size("row")):
        for yh in range(SIDE):
            for x in range(SIDE):
                to = (yh, (x + step) % SIDE) if row % 2 == 0 else ((yh + step) % SIDE, x)
                pairs.append((row * SIDE * SIDE + yh * SIDE + x, row * SIDE * SIDE + to[0] * SIDE + to[1]))
    return lax.ppermute(value, ("row", "col"), pairs)


def pack_kernel(own_c, at_ref, amps_ref, sent_ref, own_ref):
    x, yh, core = at_ref[0], at_ref[1], at_ref[2]
    rows, nv = amps_ref.shape
    tail = SIDE * own_c - LANES
    part = rows // CHUNKS

    def source(n, kind, step):
        near, e = n // own_c, n % own_c
        ab = ((yh - near + SIDE) % SIDE) * SIDE + (x + step) % SIDE
        ba = ((yh + step) % SIDE) * SIDE + (x - near + SIDE) % SIDE
        return jnp.where(kind == 0, ab, ba) * own_c + e

    kinds = [(core, 1), (core, 2), (core, 3), (0, 0), (1, 0)]
    lane = lax.broadcasted_iota(jnp.int32, (1, LANES), 1)
    wanted = [source(lane, kind, step) for kind, step in kinds]
    ends = jnp.full((1, LANES), -1, jnp.int32)
    for i, (kind, step) in enumerate(kinds):
        here = (lane >= i * tail) & (lane < (i + 1) * tail)
        ends = jnp.where(here, source(lane - i * tail + LANES, kind, step), ends)
    wanted = jnp.concatenate(wanted + [ends], 1)
    chosen = lax.broadcasted_iota(jnp.int32, (nv, wanted.shape[1]), 0) == wanted
    chosen = jnp.where(chosen, 1.0, 0.0).astype(jnp.bfloat16)

    def one(k, carry):
        at = pl.multiple_of(k * part, 16)
        got = jnp.dot(amps_ref[pl.ds(at, part), :], chosen, preferred_element_type=jnp.float32)
        end = got[:, 5 * LANES :]
        for i in range(3):
            sent_ref[i, pl.ds(at, part), :] = got[:, i * LANES : (i + 1) * LANES].astype(jnp.bfloat16)
        for i in (3, 4):
            own_ref[i - 3, pl.ds(at, part), :LANES] = got[:, i * LANES : (i + 1) * LANES].astype(jnp.bfloat16)
            own_ref[i - 3, pl.ds(at, part), LANES:] = pltpu.roll(end, LANES - i * tail, 1)[:, :tail].astype(jnp.bfloat16)
        new = []
        for i in range(3):
            turned = pltpu.roll(end, (k * tail + LANES - i * tail) % LANES, 1)
            new.append(jnp.where((lane >= k * tail) & (lane < (k + 1) * tail), turned, carry[i]))
        return tuple(new)

    carry = tuple(jnp.zeros((part, LANES), jnp.float32) for _ in range(3))
    for k in range(CHUNKS):
        carry = one(k, carry)
    for i in range(3):
        sent_ref[i, rows:, :] = carry[i].astype(jnp.bfloat16)


def unpack_kernel(pairs_p, core_ref, own_ref, mine_ref, other_ref, ab_ref, ba_ref, main, end, turned_main, turned_end):
    core = core_ref[0]
    rows, wide = ab_ref.shape[1:]
    part = rows // CHUNKS
    tail = wide - LANES

    def put(ab_from, ba_from):
        for s in range(3):
            ab_ref[s + 1, :, :LANES] = ab_from[s, :rows, :]
            main[(s + 1) * rows : (s + 2) * rows, :] = ba_from[s, :rows, :].astype(jnp.float32)
            ab_end = ab_from[s, rows:, :].astype(jnp.float32)
            ba_end = ba_from[s, rows:, :].astype(jnp.float32)
            for k in range(CHUNKS):
                shift = (LANES - k * tail) % LANES
                at = k * part
                ab_ref[s + 1, at : at + part, LANES:] = pltpu.roll(ab_end, shift, 1)[:, :tail].astype(jnp.bfloat16)
                at += (s + 1) * rows
                end[at : at + part, :] = pltpu.roll(ba_end, shift, 1)

    ab_ref[0] = own_ref[0]
    main[:rows, :] = own_ref[1, :, :LANES].astype(jnp.float32)
    end[:rows, :tail] = own_ref[1, :, LANES:].astype(jnp.float32)

    @pl.when(core == 0)
    def _():
        put(mine_ref, other_ref)

    @pl.when(core == 1)
    def _():
        put(other_ref, mine_ref)

    def one(p, carry):
        body = jnp.concatenate([main[pl.ds(p, wide, stride=pairs_p), :].T, end[pl.ds(p, wide, stride=pairs_p), :].T[:tail]], 0)
        turned_main[pl.ds(p, wide, stride=pairs_p), :] = body[:, :LANES]
        turned_end[pl.ds(p, wide, stride=pairs_p), :tail] = body[:, LANES:]
        return carry

    lax.fori_loop(0, pairs_p, one, 0, unroll=True)
    for s in range(SIDE):
        ba_ref[s, :, :LANES] = turned_main[s * rows : (s + 1) * rows, :].astype(jnp.bfloat16)
        ba_ref[s, :, LANES:] = turned_end[s * rows : (s + 1) * rows, :tail].astype(jnp.bfloat16)


def join_kernel(first, second, third, *rest):
    out_ref = rest[-1]
    for i, ref in enumerate((first, second, third)):
        out_ref[i] = ref[...]


def one_hot(shape, row_of, column_of, dtype):
    row = lax.broadcasted_iota(jnp.int32, shape, 0)
    column = lax.broadcasted_iota(jnp.int32, shape, 1)
    return jnp.where(row_of(row) == column_of(column), 1.0, 0.0).astype(dtype)


def ladder_kernel(own_a, own_c, pairs_p, core_ref, *refs):
    core = core_ref[0]
    distance = (0, 1 + 2 * core, 2, 3 - 2 * core)
    lines, partners = refs[:SIDE], refs[SIDE : 2 * SIDE]
    ab_ref, ba_ref, out_ref, window, tile, total = refs[2 * SIDE :]
    wide = SIDE * own_c
    high = GROUP * own_a
    shape = (wide, SIDE * WIN * own_c)
    row = lax.broadcasted_iota(jnp.int32, shape, 0)
    column = lax.broadcasted_iota(jnp.int32, shape, 1)
    arrived = column // (WIN * own_c)
    far = jnp.where(arrived == 1, distance[1], jnp.where(arrived == 3, distance[3], arrived))
    kept = (column % own_c + far * own_c) == row
    held = jnp.concatenate([partner[...] for partner in partners], 0)
    every = jnp.concatenate([line[...] for line in lines], 0)
    for j in range(WIN):
        place = jnp.where(kept & (column // own_c % WIN == j), 1.0, 0.0).astype(jnp.bfloat16)
        window[...] = jnp.dot(place, held, preferred_element_type=jnp.float32).astype(jnp.bfloat16)
        v = lax.dot_general(every, window[...], ROWS_BY_ROWS, preferred_element_type=jnp.float32)
        tile[:, j] = v.astype(jnp.bfloat16).reshape(SIDE * own_c // GROUP, high, wide)
    total[...] = jnp.zeros_like(total)
    groups = own_c // GROUP
    for s in range(SIDE):
        for i, amps in enumerate((ab_ref, ba_ref)):
            more = total[i]
            for g in range(groups):
                v = tile[s * groups + g].reshape(WIN * high, wide)
                part = amps[distance[s], g * GROUP * pairs_p : (g + 1) * GROUP * pairs_p, :]
                more += lax.dot_general(v, part, ROWS_BY_ROWS, preferred_element_type=jnp.float32)
            total[i] = more
    shape = total.shape[1:]
    row = lax.broadcasted_iota(jnp.int32, shape, 0)
    column = lax.broadcasted_iota(jnp.int32, shape, 1)
    same = (row % high) // own_a == column // pairs_p
    fold = one_hot((own_a * WIN, shape[0]), lambda r: r, lambda c: (c % own_a) * WIN + c // high, jnp.float32)
    out = 0.0
    for i in range(2):
        to = one_hot((shape[1], LANES), lambda r: r % pairs_p + i * pairs_p, lambda c: c, jnp.float32)
        out += jnp.dot(jnp.where(same, total[i], 0.0), to, precision=HIGHEST, preferred_element_type=jnp.float32)
    out_ref[...] = jnp.dot(fold, out, precision=HIGHEST, preferred_element_type=jnp.float32)


def add_kernel(pairs_p, parts_ref, ab_ref, ba_ref):
    total = jnp.sum(parts_ref[...], axis=0)
    ab_ref[...] = total[:, :pairs_p]
    ba_ref[...] = pltpu.roll(total, LANES - pairs_p, 1)[:, :pairs_p]


def shards(df_blocks, amplitudes):
    own_a, own_c, aux = df_blocks.shape
    pairs_p, _, nv = amplitudes.shape
    bf16, f32 = jnp.bfloat16, jnp.float32
    vmem, smem, hbm = pl.BlockSpec(memory_space=pltpu.VMEM), pl.BlockSpec(memory_space=pltpu.SMEM), pl.BlockSpec(memory_space=pl.ANY)
    params = pltpu.CompilerParams(vmem_limit_bytes=48 * 1024 * 1024)
    rows, wide = own_c * pairs_p, SIDE * own_c
    place, core = lax.axis_index("col"), lax.axis_index("row") % 2
    at = jnp.stack([place % SIDE, place // SIDE, core]).astype(jnp.int32)

    partner = from_next_row(df_blocks[:WIN].reshape(WIN * own_c, aux))
    resident = jnp.transpose(df_blocks, (1, 0, 2)).reshape(own_c * own_a, aux)
    amps = jnp.transpose(amplitudes, (1, 0, 2)).reshape(rows, nv)
    sent, own = pl.pallas_call(
        functools.partial(pack_kernel, own_c),
        out_shape=(jax.ShapeDtypeStruct((3, rows + rows // CHUNKS, LANES), bf16), jax.ShapeDtypeStruct((2, rows, wide), bf16)),
        in_specs=[smem, vmem],
        out_specs=(vmem, vmem),
        compiler_params=params,
        name="pack",
    )(at, amps)
    lines = gathered(resident, 1, 0)
    mine = [core_0_along_x_core_1_along_y(sent[s - 1], s) for s in (1, 2, 3)]
    partners = gathered(partner, 0, 1)
    mine = pl.pallas_call(
        join_kernel,
        out_shape=jax.ShapeDtypeStruct(sent.shape, bf16),
        in_specs=[vmem] * 3 + [hbm] * 3,
        out_specs=vmem,
        compiler_params=params,
        name="join",
    )(*mine, lines[1], lines[3], partners[1])
    other = between_cores(mine)
    ab, ba = pl.pallas_call(
        functools.partial(unpack_kernel, pairs_p),
        out_shape=(jax.ShapeDtypeStruct((SIDE, rows, wide), bf16),) * 2,
        in_specs=[smem, vmem, vmem, vmem],
        out_specs=(vmem, vmem),
        scratch_shapes=[pltpu.VMEM((SIDE * rows, LANES), f32)] * 4,
        compiler_params=params,
        name="unpack",
    )(at[2:], own, mine, other)
    part = pl.pallas_call(
        functools.partial(ladder_kernel, own_a, own_c, pairs_p),
        out_shape=jax.ShapeDtypeStruct((own_a * WIN, LANES), f32),
        in_specs=[smem] + [vmem] * (2 * SIDE + 2),
        out_specs=vmem,
        scratch_shapes=[
            pltpu.VMEM((wide, aux), bf16),
            pltpu.VMEM((wide // GROUP, WIN, GROUP * own_a, wide), bf16),
            pltpu.VMEM((2, WIN * GROUP * own_a, GROUP * pairs_p), f32),
        ],
        compiler_params=params,
        name="ladders",
    )(at[2:], *lines, *partners, ab, ba)
    parts = lax.all_to_all(jnp.broadcast_to(part, (SIDE * SIDE, *part.shape)), "col", 0, 0, tiled=True)
    ab, ba = pl.pallas_call(
        functools.partial(add_kernel, pairs_p),
        out_shape=(jax.ShapeDtypeStruct((own_a * WIN, pairs_p), f32),) * 2,
        in_specs=[vmem],
        out_specs=(vmem, vmem),
        compiler_params=params,
        name="add",
    )(parts)
    return ab.reshape(own_a, WIN, pairs_p), ba.reshape(own_a, WIN, pairs_p)


def solution(mesh):
    in_specs = (P("row", "col", None), P(None, "col", None))
    out_specs = (P("row", None, None), P("row", None, None))
    return jax.shard_map(shards, mesh=mesh, in_specs=in_specs, out_specs=out_specs, check_vma=False)
```

```python
import functools

import jax
import jax.numpy as jnp
from jax import lax
from jax.experimental import pallas as pl
from jax.experimental.pallas import tpu as pltpu
from jax.sharding import PartitionSpec as P

WIN = 4
SIDE = 4
LANES = 128
CHUNKS = 6
GROUP = 4
HIGHEST = lax.Precision.HIGHEST
ROWS_BY_ROWS = (((1,), (1,)), ((), ()))


def moved(value, dx, dy):
    pairs = []
    for row in range(lax.axis_size("row")):
        sign = 1 - 2 * (row % 2)
        for yh in range(SIDE):
            for x in range(SIDE):
                to = (yh + sign * dy) % SIDE * SIDE + (x + sign * dx) % SIDE
                pairs.append(((row * SIDE + yh) * SIDE + x, row * SIDE * SIDE + to))
    return lax.ppermute(value, ("row", "col"), pairs)


def gathered(value, dx, dy):
    first = moved(value, dx, dy)
    return [value, first, moved(first, dx, dy), moved(value, -dx, -dy)]


def from_next_row(value):
    rows = lax.axis_size("row")
    return lax.ppermute(value, "row", [(source, (source - 1) % rows) for source in range(rows)])


def between_cores(value):
    rows = lax.axis_size("row")
    return lax.ppermute(value, "row", [(source, source ^ 1) for source in range(rows)])


def core_0_along_x_core_1_along_y(value, step):
    pairs = []
    for row in range(lax.axis_size("row")):
        for yh in range(SIDE):
            for x in range(SIDE):
                to = (yh, (x + step) % SIDE) if row % 2 == 0 else ((yh + step) % SIDE, x)
                pairs.append((row * SIDE * SIDE + yh * SIDE + x, row * SIDE * SIDE + to[0] * SIDE + to[1]))
    return lax.ppermute(value, ("row", "col"), pairs)


def pack_kernel(own_c, at_ref, amps_ref, sent_ref, own_ref):
    x, yh, core = at_ref[0], at_ref[1], at_ref[2]
    rows, nv = amps_ref.shape
    tail = SIDE * own_c - LANES
    part = rows // CHUNKS

    def source(n, kind, step):
        near, e = n // own_c, n % own_c
        ab = ((yh - near + SIDE) % SIDE) * SIDE + (x + step) % SIDE
        ba = ((yh + step) % SIDE) * SIDE + (x - near + SIDE) % SIDE
        return jnp.where(kind == 0, ab, ba) * own_c + e

    kinds = [(core, 1), (core, 2), (core, 3), (0, 0), (1, 0)]
    lane = lax.broadcasted_iota(jnp.int32, (1, LANES), 1)
    wanted = [source(lane, kind, step) for kind, step in kinds]
    ends = jnp.full((1, LANES), -1, jnp.int32)
    for i, (kind, step) in enumerate(kinds):
        here = (lane >= i * tail) & (lane < (i + 1) * tail)
        ends = jnp.where(here, source(lane - i * tail + LANES, kind, step), ends)
    wanted = jnp.concatenate(wanted + [ends], 1)
    chosen = lax.broadcasted_iota(jnp.int32, (nv, wanted.shape[1]), 0) == wanted
    chosen = jnp.where(chosen, 1.0, 0.0).astype(jnp.bfloat16)

    def one(k, carry):
        at = pl.multiple_of(k * part, 16)
        got = jnp.dot(amps_ref[pl.ds(at, part), :], chosen, preferred_element_type=jnp.float32)
        end = got[:, 5 * LANES :]
        for i in range(3):
            sent_ref[i, pl.ds(at, part), :] = got[:, i * LANES : (i + 1) * LANES].astype(jnp.bfloat16)
        for i in (3, 4):
            own_ref[i - 3, pl.ds(at, part), :LANES] = got[:, i * LANES : (i + 1) * LANES].astype(jnp.bfloat16)
            own_ref[i - 3, pl.ds(at, part), LANES:] = pltpu.roll(end, LANES - i * tail, 1)[:, :tail].astype(jnp.bfloat16)
        new = []
        for i in range(3):
            turned = pltpu.roll(end, (k * tail + LANES - i * tail) % LANES, 1)
            new.append(jnp.where((lane >= k * tail) & (lane < (k + 1) * tail), turned, carry[i]))
        return tuple(new)

    carry = tuple(jnp.zeros((part, LANES), jnp.float32) for _ in range(3))
    for k in range(CHUNKS):
        carry = one(k, carry)
    for i in range(3):
        sent_ref[i, rows:, :] = carry[i].astype(jnp.bfloat16)


def unpack_kernel(pairs_p, core_ref, own_ref, mine_ref, other_ref, ab_ref, ba_ref, main, end, turned_main, turned_end):
    core = core_ref[0]
    rows, wide = ab_ref.shape[1:]
    part = rows // CHUNKS
    tail = wide - LANES

    def put(ab_from, ba_from):
        for s in range(3):
            ab_ref[s + 1, :, :LANES] = ab_from[s, :rows, :]
            main[(s + 1) * rows : (s + 2) * rows, :] = ba_from[s, :rows, :].astype(jnp.float32)
            ab_end = ab_from[s, rows:, :].astype(jnp.float32)
            ba_end = ba_from[s, rows:, :].astype(jnp.float32)
            for k in range(CHUNKS):
                shift = (LANES - k * tail) % LANES
                at = k * part
                ab_ref[s + 1, at : at + part, LANES:] = pltpu.roll(ab_end, shift, 1)[:, :tail].astype(jnp.bfloat16)
                at += (s + 1) * rows
                end[at : at + part, :] = pltpu.roll(ba_end, shift, 1)

    ab_ref[0] = own_ref[0]
    main[:rows, :] = own_ref[1, :, :LANES].astype(jnp.float32)
    end[:rows, :tail] = own_ref[1, :, LANES:].astype(jnp.float32)

    @pl.when(core == 0)
    def _():
        put(mine_ref, other_ref)

    @pl.when(core == 1)
    def _():
        put(other_ref, mine_ref)

    def one(p, carry):
        body = jnp.concatenate([main[pl.ds(p, wide, stride=pairs_p), :].T, end[pl.ds(p, wide, stride=pairs_p), :].T[:tail]], 0)
        turned_main[pl.ds(p, wide, stride=pairs_p), :] = body[:, :LANES]
        turned_end[pl.ds(p, wide, stride=pairs_p), :tail] = body[:, LANES:]
        return carry

    lax.fori_loop(0, pairs_p, one, 0, unroll=16)
    for s in range(SIDE):
        ba_ref[s, :, :LANES] = turned_main[s * rows : (s + 1) * rows, :].astype(jnp.bfloat16)
        ba_ref[s, :, LANES:] = turned_end[s * rows : (s + 1) * rows, :tail].astype(jnp.bfloat16)


def join_kernel(first, second, third, *rest):
    out_ref = rest[-1]
    for i, ref in enumerate((first, second, third)):
        out_ref[i] = ref[...]


def one_hot(shape, row_of, column_of, dtype):
    row = lax.broadcasted_iota(jnp.int32, shape, 0)
    column = lax.broadcasted_iota(jnp.int32, shape, 1)
    return jnp.where(row_of(row) == column_of(column), 1.0, 0.0).astype(dtype)


def ladder_kernel(own_a, own_c, pairs_p, core_ref, *refs):
    core = core_ref[0]
    distance = (0, 1 + 2 * core, 2, 3 - 2 * core)
    lines, partners = refs[:SIDE], refs[SIDE : 2 * SIDE]
    ab_ref, ba_ref, out_ref, window, tile, total = refs[2 * SIDE :]
    wide = SIDE * own_c
    high = GROUP * own_a
    shape = (wide, SIDE * WIN * own_c)
    row = lax.broadcasted_iota(jnp.int32, shape, 0)
    column = lax.broadcasted_iota(jnp.int32, shape, 1)
    arrived = column // (WIN * own_c)
    far = jnp.where(arrived == 1, distance[1], jnp.where(arrived == 3, distance[3], arrived))
    kept = (column % own_c + far * own_c) == row
    held = jnp.concatenate([partner[...] for partner in partners], 0)
    every = jnp.concatenate([line[...] for line in lines], 0)
    for j in range(WIN):
        place = jnp.where(kept & (column // own_c % WIN == j), 1.0, 0.0).astype(jnp.bfloat16)
        window[...] = jnp.dot(place, held, preferred_element_type=jnp.float32).astype(jnp.bfloat16)
        v = lax.dot_general(every, window[...], ROWS_BY_ROWS, preferred_element_type=jnp.float32)
        tile[:, j] = v.astype(jnp.bfloat16).reshape(SIDE * own_c // GROUP, high, wide)
    total[...] = jnp.zeros_like(total)
    groups = own_c // GROUP
    for s in range(SIDE):
        for i, amps in enumerate((ab_ref, ba_ref)):
            more = total[i]
            for g in range(groups):
                v = tile[s * groups + g].reshape(WIN * high, wide)
                part = amps[distance[s], g * GROUP * pairs_p : (g + 1) * GROUP * pairs_p, :]
                more += lax.dot_general(v, part, ROWS_BY_ROWS, preferred_element_type=jnp.float32)
            total[i] = more
    shape = total.shape[1:]
    row = lax.broadcasted_iota(jnp.int32, shape, 0)
    column = lax.broadcasted_iota(jnp.int32, shape, 1)
    same = (row % high) // own_a == column // pairs_p
    fold = one_hot((own_a * WIN, shape[0]), lambda r: r, lambda c: (c % own_a) * WIN + c // high, jnp.float32)
    out = 0.0
    for i in range(2):
        to = one_hot((shape[1], LANES), lambda r: r % pairs_p + i * pairs_p, lambda c: c, jnp.float32)
        out += jnp.dot(jnp.where(same, total[i], 0.0), to, precision=HIGHEST, preferred_element_type=jnp.float32)
    out_ref[...] = jnp.dot(fold, out, precision=HIGHEST, preferred_element_type=jnp.float32)


def add_kernel(pairs_p, parts_ref, ab_ref, ba_ref):
    total = jnp.sum(parts_ref[...], axis=0)
    ab_ref[...] = total[:, :pairs_p]
    ba_ref[...] = pltpu.roll(total, LANES - pairs_p, 1)[:, :pairs_p]


def shards(df_blocks, amplitudes):
    own_a, own_c, aux = df_blocks.shape
    pairs_p, _, nv = amplitudes.shape
    bf16, f32 = jnp.bfloat16, jnp.float32
    vmem, smem, hbm = pl.BlockSpec(memory_space=pltpu.VMEM), pl.BlockSpec(memory_space=pltpu.SMEM), pl.BlockSpec(memory_space=pl.ANY)
    params = pltpu.CompilerParams(vmem_limit_bytes=48 * 1024 * 1024)
    rows, wide = own_c * pairs_p, SIDE * own_c
    place, core = lax.axis_index("col"), lax.axis_index("row") % 2
    at = jnp.stack([place % SIDE, place // SIDE, core]).astype(jnp.int32)

    partner = from_next_row(df_blocks[:WIN].reshape(WIN * own_c, aux))
    resident = jnp.transpose(df_blocks, (1, 0, 2)).reshape(own_c * own_a, aux)
    amps = jnp.transpose(amplitudes, (1, 0, 2)).reshape(rows, nv)
    sent, own = pl.pallas_call(
        functools.partial(pack_kernel, own_c),
        out_shape=(jax.ShapeDtypeStruct((3, rows + rows // CHUNKS, LANES), bf16), jax.ShapeDtypeStruct((2, rows, wide), bf16)),
        in_specs=[smem, vmem],
        out_specs=(vmem, vmem),
        compiler_params=params,
        name="pack",
    )(at, amps)
    lines = gathered(resident, 1, 0)
    mine = [core_0_along_x_core_1_along_y(sent[s - 1], s) for s in (1, 2, 3)]
    partners = gathered(partner, 0, 1)
    mine = pl.pallas_call(
        join_kernel,
        out_shape=jax.ShapeDtypeStruct(sent.shape, bf16),
        in_specs=[vmem] * 3 + [hbm] * 2,
        out_specs=vmem,
        compiler_params=params,
        name="join",
    )(*mine, lines[1], partners[1])
    other = between_cores(mine)
    ab, ba = pl.pallas_call(
        functools.partial(unpack_kernel, pairs_p),
        out_shape=(jax.ShapeDtypeStruct((SIDE, rows, wide), bf16),) * 2,
        in_specs=[smem, vmem, vmem, vmem],
        out_specs=(vmem, vmem),
        scratch_shapes=[pltpu.VMEM((SIDE * rows, LANES), f32)] * 4,
        compiler_params=params,
        name="unpack",
    )(at[2:], own, mine, other)
    part = pl.pallas_call(
        functools.partial(ladder_kernel, own_a, own_c, pairs_p),
        out_shape=jax.ShapeDtypeStruct((own_a * WIN, LANES), f32),
        in_specs=[smem] + [vmem] * (2 * SIDE + 2),
        out_specs=vmem,
        scratch_shapes=[
            pltpu.VMEM((wide, aux), bf16),
            pltpu.VMEM((wide // GROUP, WIN, GROUP * own_a, wide), bf16),
            pltpu.VMEM((2, WIN * GROUP * own_a, GROUP * pairs_p), f32),
        ],
        compiler_params=params,
        name="ladders",
    )(at[2:], *lines, *partners, ab, ba)
    parts = lax.all_to_all(jnp.broadcast_to(part, (SIDE * SIDE, *part.shape)), "col", 0, 0, tiled=True)
    ab, ba = pl.pallas_call(
        functools.partial(add_kernel, pairs_p),
        out_shape=(jax.ShapeDtypeStruct((own_a * WIN, pairs_p), f32),) * 2,
        in_specs=[vmem],
        out_specs=(vmem, vmem),
        compiler_params=params,
        name="add",
    )(parts)
    return ab.reshape(own_a, WIN, pairs_p), ba.reshape(own_a, WIN, pairs_p)


def solution(mesh):
    in_specs = (P("row", "col", None), P(None, "col", None))
    out_specs = (P("row", None, None), P("row", None, None))
    return jax.shard_map(shards, mesh=mesh, in_specs=in_specs, out_specs=out_specs, check_vma=False)
```
